32 devices in a mesh: ctx: 16 (over z, y, core), tp: 2 (over x).
Axes of the slice: x: 2, y: 2, z: 4, core: 2. Of those that a mesh axis runs over, the one named last changes fastest.
Arguments:
- hidden_in: bfloat16 [4096, 2048], P('ctx', 'tp'), may hold values from -6 to 6
- ln_gain: float32 [2048], replicated, may hold values from 0.1 to 1.9
- ln_bias: float32 [2048], replicated, may hold values from -3 to 3
- w_qkv: bfloat16 [3, 2048, 2048], P(None, None, 'tp')
- w_out: bfloat16 [2048, 2048], P('tp'), may hold values from -0.375 to 0.375
- segment_ids: int32 [4096], P('ctx'), may hold values from 0 to 2, as said below
- prompt_lengths: int32 [3], replicated, may hold values from 1 to 2048, as said below
- page_table: int32 [3, 16], replicated, may hold values from -1 to 79, as said below
Outputs:
- attn_out: bfloat16 [4096, 2048], P('ctx', 'tp')
- kv_cache: bfloat16 [80, 128, 2, 2048], P('ctx', None, None, 'tp')
The draws below stay inside these ranges and needn't reach their ends.
Inputs may be any that keep to these rules, and one draw needn't show every extreme that they name: `segment_ids`: each prompt's tokens are consecutive and the numbers never fall along the tokens; prompt i holds exactly prompt_lengths[i] tokens. `prompt_lengths`: the lengths sum to 4096; prompt 0 is shorter than 256 tokens and not a multiple of 128; prompt 1 is the longest, exactly 2048 tokens. `page_table`: for page j of prompt i with j * 128 below prompt_lengths[i], the entry is owner * 5 + slot with slot below 5, where owner is the ctx index whose tokens include the page's first token, starts_i + j * 128; distinct pages have distinct entries; all other entries are -1.
All inputs are finite; a program needn't handle non-finite values.
Results may differ from the reference program's by a relative error of at most 0.013.
Values may be sent and summed in bfloat16 or wider, within the bound.
No kernel may reach another device: no remote copies, remote signals or barrier semaphores. Data moves between devices by JAX's collectives and lax.ppermute only.
A program may use at most 128 MiB of HBM per device.

```python
import math
import jax
import jax.numpy as jnp
from jax import lax

D = 2048
H = 8
HD = 256
TOK_DEV = 256
PAGE = 128
NSEG = 3
SPAN = 8
TOKENS = 4096
MAXPAGES = 16
SLOTS = 5
CACHE_SLOTS = 80
N_CTX = 16
N_TP = 2


def segment_layout(key):
    base_key = jax.random.fold_in(key, 101)
    longest = SPAN * TOK_DEV
    whole_pages = jax.random.randint(jax.random.fold_in(base_key, 1), (), 0, TOK_DEV // PAGE).astype(jnp.int32)
    extra_part = jax.random.randint(jax.random.fold_in(base_key, 2), (), 1, PAGE).astype(jnp.int32)
    first_length = (whole_pages * PAGE + extra_part).astype(jnp.int32)
    starts = jnp.stack([jnp.zeros((), jnp.int32), first_length, first_length + longest]).astype(jnp.int32)
    finish = jnp.concatenate([starts[1:], jnp.full((1,), TOKENS, jnp.int32)])
    lengths = (finish - starts).astype(jnp.int32)
    token_index = jnp.arange(TOKENS, dtype=jnp.int32)
    segment_ids = (jnp.sum((starts[None, :] <= token_index[:, None]).astype(jnp.int32), axis=1) - 1).astype(jnp.int32)
    page_index = jnp.arange(MAXPAGES, dtype=jnp.int32)
    page_first = starts[:, None] + page_index[None, :] * PAGE
    is_valid = page_index[None, :] * PAGE < lengths[:, None]
    page_owner = page_first // TOK_DEV
    flat_first = page_first.reshape(-1)
    flat_owner = page_owner.reshape(-1)
    flat_valid = is_valid.reshape(-1)
    earlier = flat_valid[None, :] & (flat_owner[None, :] == flat_owner[:, None]) & (flat_first[None, :] < flat_first[:, None])
    page_rank = jnp.sum(earlier.astype(jnp.int32), axis=1)
    orders = jax.vmap(lambda subkey: jax.random.permutation(subkey, SLOTS))(jax.random.split(jax.random.fold_in(base_key, 3), N_CTX)).astype(jnp.int32)
    slot_pick = orders[jnp.clip(flat_owner, 0, N_CTX - 1), jnp.clip(page_rank, 0, SLOTS - 1)]
    page_map = jnp.where(flat_valid, flat_owner * SLOTS + slot_pick, -1).astype(jnp.int32).reshape(NSEG, MAXPAGES)
    return (segment_ids, lengths, page_map)


def draw_segment_ids(key, part):
    return segment_layout(key)[0]


def draw_prompt_lengths(key, part):
    return segment_layout(key)[1]


def draw_page_table(key, part):
    return segment_layout(key)[2]


def draw_w_qkv(key, part):
    drawn_draw = jax.random.normal(jax.random.fold_in(key, 201), (3, D, H * HD), jnp.float32) * D ** (-0.5)
    return drawn_draw.astype(jnp.bfloat16)


def steps_of(own_key, dims, pieces, low, top_value):
    gain = 1.0
    for position, parts in pieces:
        steps = jax.random.uniform(jax.random.fold_in(jax.random.fold_in(own_key, 6), position), (parts,), jnp.float32, low / len(pieces), top_value / len(pieces))
        gain = gain * jnp.repeat(jnp.exp(steps), dims[position] // parts).reshape((-1,) + (1,) * (len(dims) - 1 - position))
    return gain


def centred(key, extent, width, bound, cuts=(), kind=jnp.bfloat16):
    array = jax.random.normal(key, extent, jnp.float32) * width
    if len(cuts) > 0:
        array = steps_of(key, extent, cuts, -0.22, 0.18) * array
    return jnp.clip(array, min=-bound, max=bound).astype(kind)


def setup_inputs(seed: int = 0) -> dict:
    keys = jax.random.split(jax.random.key(seed), 9)
    hidden_in = centred(keys[0], (TOKENS, D), 1.0, 6.0, ((0, 16), (1, 2)))
    ln_gain = jnp.clip(1.0 + 0.18 * jax.random.normal(keys[1], (D,), jnp.float32), 0.1, 1.9)
    ln_bias = centred(keys[2], (D,), 0.5, 3.0, (), jnp.float32)
    w_qkv = draw_w_qkv(jax.random.fold_in(keys[8], 71), 0)
    w_out = centred(keys[4], (H * HD, D), HD ** -0.5, 0.375, ((0, 2),))
    segment_ids = draw_segment_ids(jax.random.fold_in(keys[8], 71), 0)
    prompt_lengths = draw_prompt_lengths(jax.random.fold_in(keys[8], 71), 0)
    page_table = draw_page_table(jax.random.fold_in(keys[8], 71), 0)
    return dict(hidden_in=hidden_in, ln_gain=ln_gain, ln_bias=ln_bias, w_qkv=w_qkv, w_out=w_out, segment_ids=segment_ids, prompt_lengths=prompt_lengths, page_table=page_table)


EPSILON = 1e-05

def normalize(inputs, norm_gain, norm_bias):
    average = lax.optimization_barrier(jnp.sum(inputs, axis=-1, keepdims=True)) / inputs.shape[-1]
    centered = inputs - average
    spread = lax.optimization_barrier(jnp.sum(centered * centered, axis=-1, keepdims=True)) / inputs.shape[-1]
    return centered * lax.rsqrt(spread + EPSILON) * norm_gain + norm_bias

def rotary(inputs, positions):
    quarter = inputs.shape[-1] // 4
    halfway = quarter // 2
    exponent = jnp.arange(0, quarter, 2).astype(jnp.float32) / quarter
    inverse = jnp.power(jnp.float32(10000.0), -exponent)
    angles = positions.astype(jnp.float32)[:, None] * inverse[None, :]
    cosine_table = jnp.concatenate([jnp.cos(angles), jnp.cos(angles)], axis=-1)[:, None, :]
    sine_table = jnp.concatenate([jnp.sin(angles), jnp.sin(angles)], axis=-1)[:, None, :]
    leading = inputs[..., :quarter]
    turned = jnp.concatenate([-leading[..., halfway:], leading[..., :halfway]], axis=-1)
    return jnp.concatenate([leading * cosine_table + turned * sine_table, inputs[..., quarter:]], axis=-1)

def reference(hidden_in, ln_gain, ln_bias, w_qkv, w_out, segment_ids, prompt_lengths, page_table):
    normed = normalize(hidden_in.astype(jnp.float32), ln_gain, ln_bias).astype(jnp.bfloat16)
    starts = (jnp.cumsum(prompt_lengths) - prompt_lengths).astype(jnp.int32)
    positions = (jnp.arange(TOKENS, dtype=jnp.int32) - starts[segment_ids]).astype(jnp.int32)
    query_heads = rotary(jnp.dot(normed, w_qkv[0], preferred_element_type=jnp.float32).reshape(TOKENS, H, HD), positions).astype(jnp.bfloat16)
    key_heads = rotary(jnp.dot(normed, w_qkv[1], preferred_element_type=jnp.float32).reshape(TOKENS, H, HD), positions).astype(jnp.bfloat16)
    value_heads = jnp.dot(normed, w_qkv[2], preferred_element_type=jnp.float32).reshape(TOKENS, H, HD).astype(jnp.bfloat16)
    reach_rows = SPAN * TOK_DEV
    padded_keys = jnp.concatenate([jnp.zeros((reach_rows, H, HD), jnp.bfloat16), key_heads], axis=0)
    padded_values = jnp.concatenate([jnp.zeros((reach_rows, H, HD), jnp.bfloat16), value_heads], axis=0)
    padded_marks = jnp.concatenate([jnp.full((reach_rows,), -1, jnp.int32), segment_ids], axis=0)

    def attend_block(block_number):
        first_row = (block_number * TOK_DEV).astype(jnp.int32)
        query_block = lax.dynamic_slice_in_dim(query_heads, first_row, TOK_DEV, 0).astype(jnp.float32)
        query_marks = lax.dynamic_slice_in_dim(segment_ids, first_row, TOK_DEV, 0)
        key_block = lax.dynamic_slice_in_dim(padded_keys, first_row, reach_rows + TOK_DEV, 0).astype(jnp.float32)
        value_block = lax.dynamic_slice_in_dim(padded_values, first_row, reach_rows + TOK_DEV, 0).astype(jnp.float32)
        key_marks = lax.dynamic_slice_in_dim(padded_marks, first_row, reach_rows + TOK_DEV, 0)
        query_index = first_row + jnp.arange(TOK_DEV, dtype=jnp.int32)
        key_index = first_row - reach_rows + jnp.arange(reach_rows + TOK_DEV, dtype=jnp.int32)
        visible = (query_marks[:, None] == key_marks[None, :]) & (key_index[None, :] <= query_index[:, None])
        scores = jnp.einsum('qhd,khd->hqk', query_block, key_block) / math.sqrt(HD)
        scores = jnp.where(visible[None], scores, -jnp.inf)
        row_peak = lax.optimization_barrier(jnp.max(scores, axis=-1, keepdims=True))
        weights = jnp.exp(scores - row_peak).astype(jnp.bfloat16)
        weights = lax.optimization_barrier(weights).astype(jnp.float32)
        totals = lax.optimization_barrier(jnp.sum(weights, axis=-1))
        mixture = jnp.einsum('hqk,khd->hqd', weights, value_block) / totals[..., None]
        return jnp.transpose(mixture, (1, 0, 2)).astype(jnp.bfloat16)
    attended = lax.map(attend_block, jnp.arange(N_CTX, dtype=jnp.int32)).reshape(TOKENS, H * HD)
    group_width = H // N_TP * HD
    accumulated = jnp.zeros((TOKENS, D), jnp.float32)
    for member in range(N_TP):
        partial_value = jnp.dot(attended[:, member * group_width:(member + 1) * group_width], w_out[member * group_width:(member + 1) * group_width], preferred_element_type=jnp.float32).astype(jnp.bfloat16)
        accumulated = accumulated + lax.optimization_barrier(partial_value).astype(jnp.float32)
    attn_out = accumulated.astype(jnp.bfloat16)
    page_slot = page_table[segment_ids, positions // PAGE]
    offsets = positions % PAGE
    kv_cache = jnp.zeros((CACHE_SLOTS, PAGE, 2, H * HD), jnp.bfloat16)
    kv_cache = kv_cache.at[page_slot, offsets, 0].set(key_heads.reshape(TOKENS, H * HD))
    kv_cache = kv_cache.at[page_slot, offsets, 1].set(value_heads.reshape(TOKENS, H * HD))
    return (attn_out, kv_cache)
```

```python
import functools
import math

import jax
import jax.numpy as jnp
from jax import lax
from jax.experimental import pallas as pl
from jax.experimental.pallas import tpu as pltpu
from jax.sharding import PartitionSpec as P

HD = 256
PAGE = 128
EPSILON = 1e-05
ROT = HD // 4
LANES = 128
VMEM = pltpu.VMEM
MASKED = -1e30
LOG2E = 1.4426950408889634


def start_rows(prompt_lengths):
    return (jnp.cumsum(prompt_lengths) - prompt_lengths).astype(jnp.int32)


def first_of_prompt(rows, starts):
    first = jnp.zeros_like(rows)
    for prompt in range(starts.shape[0]):
        first = jnp.where(rows >= starts[prompt], starts[prompt], first)
    return first


def rotary_tables(positions):
    exponent = jnp.arange(0, ROT, 2).astype(jnp.float32) / ROT
    inverse = jnp.power(jnp.float32(10000.0), -exponent)
    angles = positions.astype(jnp.float32)[:, None] * inverse[None, :]
    cosine, sine = jnp.cos(angles), jnp.sin(angles)
    rows, half = angles.shape
    blank = jnp.zeros((rows, LANES - 2 * half), jnp.float32)
    none = jnp.zeros_like(sine)
    keep = jnp.concatenate([cosine, cosine, blank + 1.0], axis=1)
    from_below = jnp.concatenate([none, sine, blank], axis=1)
    from_above = jnp.concatenate([-sine, none, blank], axis=1)
    return keep, from_below, from_above


def qkv_kernel(info, own, other, gain, bias, keep, below, above, weights, *refs):
    splits = (len(refs) - 4) // 2
    q_refs, kv_refs = refs[:splits], refs[splits : 2 * splits]
    keys_ref, values_ref, head_ref, normed = refs[2 * splits :]
    step = pl.program_id(0)
    width = own.shape[1]
    rank = info[1]

    @pl.when(step == 0)
    def _():
        full = 2 * width
        mine = own[...].astype(jnp.float32)
        theirs = other[...].astype(jnp.float32)
        total = jnp.sum(mine, axis=-1, keepdims=True) + jnp.sum(theirs, axis=-1, keepdims=True)
        average = total / full
        mine, theirs = mine - average, theirs - average
        spread = jnp.sum(mine * mine, axis=-1, keepdims=True) + jnp.sum(
            theirs * theirs, axis=-1, keepdims=True
        )
        scale = lax.rsqrt(spread / full + EPSILON)
        for part, place in ((mine, rank), (theirs, 1 - rank)):
            columns = pl.ds(pl.multiple_of(place * width, width), width)
            normed[:, columns] = (part * scale * gain[:, columns] + bias[:, columns]).astype(
                jnp.bfloat16
            )

    rows = normed[...]
    query, key, value = (
        jnp.dot(rows, weights[j], preferred_element_type=jnp.float32) for j in range(3)
    )

    def turned(inputs):
        leading = inputs[:, :LANES]
        leading = (
            leading * keep[...]
            + pltpu.roll(leading, ROT // 2, 1) * below[...]
            + pltpu.roll(leading, LANES - ROT // 2, 1) * above[...]
        )
        return jnp.concatenate([leading, inputs[:, LANES:]], axis=1).astype(jnp.bfloat16)

    query, key, value = turned(query), turned(key), value.astype(jnp.bfloat16)
    keys_ref[...] = key
    values_ref[...] = value
    for split in range(splits):

        @pl.when(step == split)
        def _():
            q_refs[split][...] = query
            kv_refs[split][:, :HD] = key
            kv_refs[split][:, HD:] = value

    page = head_ref.shape[1]
    head_ref[0] = key[:page]
    head_ref[1] = value[:page]


def project(info, own, other, gain, bias, tables, w_qkv, splits):
    rows, width = own.shape
    heads = w_qkv.shape[2] // HD
    whole = lambda *shape: pl.BlockSpec(shape, lambda m, info: (0,) * len(shape))
    by_head = pl.BlockSpec((rows, HD), lambda m, info: (0, info[0] ^ m))
    return pl.pallas_call(
        qkv_kernel,
        grid_spec=pltpu.PrefetchScalarGridSpec(
            num_scalar_prefetch=1,
            grid=(splits,),
            in_specs=[
                whole(rows, width),
                whole(rows, width),
                whole(1, 2 * width),
                whole(1, 2 * width),
                whole(rows, LANES),
                whole(rows, LANES),
                whole(rows, LANES),
                pl.BlockSpec((3, 2 * width, HD), lambda m, info: (0, 0, info[0] ^ m)),
            ],
            out_specs=[whole(rows, HD)] * splits
            + [whole(rows, 2 * HD)] * splits
            + [by_head, by_head, pl.BlockSpec((2, PAGE, HD), lambda m, info: (0, 0, info[0] ^ m))],
            scratch_shapes=[VMEM((rows, 2 * width), jnp.bfloat16)],
        ),
        out_shape=[jax.ShapeDtypeStruct((rows, HD), jnp.bfloat16)] * splits
        + [jax.ShapeDtypeStruct((rows, 2 * HD), jnp.bfloat16)] * splits
        + [jax.ShapeDtypeStruct((rows, heads * HD), jnp.bfloat16)] * 2
        + [jax.ShapeDtypeStruct((2, PAGE, heads * HD), jnp.bfloat16)],
        compiler_params=pltpu.CompilerParams(vmem_limit_bytes=40 * 2**20),
        cost_estimate=pl.CostEstimate(
            flops=2 * rows * 2 * width * 3 * heads * HD,
            bytes_accessed=2 * 3 * 2 * width * heads * HD,
            transcendentals=0,
        ),
        name="project",
    )(info, own, other, gain, bias, *tables, w_qkv)


def soft_attend(query, keys, values, first_key, last_key, base):
    scores = lax.dot_general(
        query, keys, (((1,), (1,)), ((), ())), preferred_element_type=jnp.float32
    )
    column = base + lax.broadcasted_iota(jnp.int32, scores.shape, 1)
    visible = (column >= first_key) & (column <= last_key)
    scores = jnp.where(visible, scores, MASKED)
    peak = jnp.max(scores, axis=-1, keepdims=True)
    factor = LOG2E / math.sqrt(HD)
    weights = jnp.exp2((scores - peak) * factor).astype(jnp.bfloat16)
    total = jnp.sum(weights.astype(jnp.float32), axis=-1, keepdims=True)
    mixed = jnp.dot(weights, values, preferred_element_type=jnp.float32) / total
    return mixed, peak * factor + jnp.log2(total)


def row_bounds(info, rows):
    first = jnp.zeros_like(rows)
    for prompt in range(3, 6):
        first = jnp.where(rows >= info[prompt], info[prompt], first)
    return first


def arrange(info, mine_refs, theirs_refs, keys, values):
    rows = mine_refs[0].shape[0]
    for refs, core in ((mine_refs, info[2]), (theirs_refs, 1 - info[2])):
        for split, ref in enumerate(refs):
            at = pl.ds(pl.multiple_of((2 * (info[0] ^ split) + core) * rows, rows), rows)
            keys[at, :] = ref[:, :HD]
            values[at, :] = ref[:, HD:]


def tail_kernel(info, *refs):
    splits = (len(refs) - 3) // 3
    queries, mine, theirs = refs[:splits], refs[splits : 2 * splits], refs[2 * splits : 3 * splits]
    out, keys, values = refs[3 * splits :]
    rows = queries[0].shape[0]

    @pl.when((info[6] == 0) & (info[2] == 0))
    def _():
        arrange(info, mine, theirs, keys, values)
        query = queries[0][...]
        for split in range(1, splits):
            query = jnp.where(info[0] == split, queries[split][...], query)
        group_rows = 2 * splits * rows
        row = group_rows + lax.broadcasted_iota(jnp.int32, (rows, 1), 0)
        first = row_bounds(info, row)
        mixed, level = soft_attend(query, keys[...], values[...], first, row, 0)
        level = jnp.where(first < group_rows, level, MASKED)
        out[:, :HD] = mixed.astype(jnp.bfloat16)
        lane = lax.broadcasted_iota(jnp.int32, (rows, LANES), 1)
        high = level.astype(jnp.bfloat16).astype(jnp.float32)
        middle = (level - high).astype(jnp.bfloat16).astype(jnp.float32)
        low = level - high - middle
        out[:, HD:] = jnp.where(
            lane == 0, high, jnp.where(lane == 1, middle, jnp.where(lane == 2, low, 0.0))
        ).astype(jnp.bfloat16)


def main_kernel(info, *refs):
    splits = (len(refs) - 6) // 4
    queries, mine, theirs = refs[:splits], refs[splits : 2 * splits], refs[2 * splits : 3 * splits]
    outs = refs[3 * splits : 4 * splits]
    first_mixed, first_level, keys, values, asked, gathered = refs[4 * splits :]
    rows = queries[0].shape[0]
    arrange(info, mine, theirs, keys, values)
    for split in range(splits):
        at = pl.ds(pl.multiple_of((info[0] ^ split) * rows, rows), rows)
        asked[at, :] = queries[split][...]
    for place in range(splits):
        reach = (2 * place + 2) * rows
        row = info[6] + (2 * place + info[2]) * rows + lax.broadcasted_iota(jnp.int32, (rows, 1), 0)
        mixed, level = soft_attend(
            asked[place * rows : (place + 1) * rows, :],
            keys[:reach, :],
            values[:reach, :],
            row_bounds(info, row),
            row,
            info[6],
        )
        gathered[place * rows : (place + 1) * rows, :] = mixed.astype(jnp.bfloat16)
        if place == 0:
            first_mixed[...] = mixed
            first_level[...] = jnp.broadcast_to(level, first_level.shape)
    for split in range(splits):
        at = pl.ds(pl.multiple_of((info[0] ^ split) * rows, rows), rows)
        outs[split][...] = gathered[at, :]


def on_core(kernel, out_shape, scratch, name, flops):
    def call(info, *operands):
        return pl.pallas_call(
            kernel,
            in_specs=[pl.BlockSpec(memory_space=pltpu.SMEM)]
            + [pl.BlockSpec(memory_space=pltpu.VMEM)] * len(operands),
            out_specs=jax.tree.map(lambda _: pl.BlockSpec(memory_space=pltpu.VMEM), out_shape),
            out_shape=out_shape,
            scratch_shapes=scratch,
            compiler_params=pltpu.CompilerParams(vmem_limit_bytes=40 * 2**20),
            cost_estimate=pl.CostEstimate(flops=flops, bytes_accessed=4 * 2**20, transcendentals=0),
            name=name,
        )(info, *operands)

    return call


def out_kernel(info, *refs):
    splits = (len(refs) - 4) // 2
    mine, theirs = refs[:splits], refs[splits : 2 * splits]
    w_own, w_same, w_swap, out = refs[2 * splits :]
    half = splits // 2
    total = jnp.zeros(out.shape, jnp.float32)
    for split in range(splits):
        head = info[0] ^ split
        at = pl.ds(pl.multiple_of(head * HD, HD), HD)
        total += jnp.dot(mine[split][...], w_own[at, :], preferred_element_type=jnp.float32)
    for split in range(splits):
        head = info[0] ^ split
        at = pl.ds(pl.multiple_of(lax.rem(head, half) * HD, HD), HD)
        same = head // half == info[2]
        weight = jnp.where(same, w_same[at, :], w_swap[at, :])
        total += jnp.dot(theirs[split][...], weight, preferred_element_type=jnp.float32)
    out[...] = total.astype(jnp.bfloat16)


def split_heads(hidden_in, ln_gain, ln_bias, w_qkv, w_out, segment_ids, prompt_lengths, page_table):
    rows, width = hidden_in.shape
    splits = w_out.shape[0] // HD
    count = lax.axis_size("ctx")
    index = lax.axis_index("ctx")
    rank = lax.axis_index("tp")
    group = 2 * splits
    core, place = index % 2, index // 2 % splits
    starts = start_rows(prompt_lengths)
    scalars = [place, rank, core, starts[0], starts[1], starts[2], index // group * group * rows, index]
    info = jnp.stack([jnp.asarray(v, jnp.int32) for v in scalars])

    def across(value, ctx_mask, tp_mask=0):
        pairs = []
        for c in range(count):
            for t in range(2):
                pairs.append((2 * c + t, 2 * (c ^ ctx_mask) + (t ^ tp_mask)))
        return lax.ppermute(value, ("ctx", "tp"), pairs)

    other = across(hidden_in, 0, 1)
    row_index = index * rows + jnp.arange(rows, dtype=jnp.int32)
    tables = rotary_tables(row_index - first_of_prompt(row_index, starts))
    results = project(
        info, hidden_in, other, ln_gain[None, :], ln_bias[None, :], tables, w_qkv, splits
    )
    queries, pairs = results[:splits], results[splits : 2 * splits]
    keys, values, page_head = results[2 * splits :]

    kv_mine = [pairs[0]] + [None] * (splits - 1)
    q_mine = [queries[0]] + [None] * (splits - 1)
    for split in reversed(range(1, splits)):
        kv_mine[split] = across(pairs[split], 2 * split)
    for split in reversed(range(1, splits)):
        q_mine[split] = across(queries[split], 2 * split)
    q_tail = [lax.ppermute(queries[s], "ctx", [(group, 2 * s)]) for s in range(splits)]
    kv_theirs = [across(kv_mine[split], 1) for split in range(splits)]

    send_rows = w_out.shape[0] // 2
    outgoing = lax.dynamic_slice(w_out, (core * send_rows, (1 - rank) * width), (send_rows, width))
    outgoing, _ = lax.optimization_barrier((outgoing, other))
    w_same = across(outgoing, 0, 1)
    w_swap = across(w_same, 1)

    scratch = [VMEM((group * rows, HD), jnp.bfloat16)] * 2
    tile = 4 * rows * rows * HD
    tail = on_core(
        tail_kernel,
        jax.ShapeDtypeStruct((rows, HD + LANES), jnp.bfloat16),
        scratch,
        "tail",
        group * tile,
    )(info, *q_tail, *kv_mine, *kv_theirs)
    far = lax.ppermute(tail, "ctx", [(2 * s, group + 2 * s) for s in range(splits)])
    attended = on_core(
        main_kernel,
        [jax.ShapeDtypeStruct((rows, HD), jnp.bfloat16)] * splits
        + [
            jax.ShapeDtypeStruct((rows, HD), jnp.float32),
            jax.ShapeDtypeStruct((rows, LANES), jnp.float32),
        ],
        scratch + [VMEM((splits * rows, HD), jnp.bfloat16)] * 2,
        "main",
        splits * (splits + 1) * tile,
    )(info, *q_mine, *kv_mine, *kv_theirs)
    blocks, near_mixed, near_level = attended[:splits], attended[splits], attended[splits + 1][:, :1]
    far_parts = far[:, HD : HD + 3].astype(jnp.float32)
    far_level = far_parts[:, :1] + far_parts[:, 1:2] + far_parts[:, 2:3]
    highest = jnp.maximum(near_level, far_level)
    near_weight, far_weight = jnp.exp2(near_level - highest), jnp.exp2(far_level - highest)
    merged = (near_mixed * near_weight + far[:, :HD].astype(jnp.float32) * far_weight) / (
        near_weight + far_weight
    )
    crossing = (index >= group) & (core == 0)
    applies = crossing & (jnp.arange(rows)[:, None] < starts[2] - group * rows)
    blocks = [
        jnp.where(applies & (place == s), merged.astype(jnp.bfloat16), blocks[s])
        for s in range(splits)
    ]

    near = [blocks[0]] + [across(blocks[s], 2 * s) for s in range(1, splits)]
    beyond = [across(blocks[s], 2 * s, 1) for s in range(splits)]
    w_blocks = w_out.shape[0]
    operands = [*near, *beyond]
    attn_out = pl.pallas_call(
        out_kernel,
        grid_spec=pltpu.PrefetchScalarGridSpec(
            num_scalar_prefetch=1,
            grid=(1,),
            in_specs=[pl.BlockSpec((rows, HD), lambda i, info: (0, 0))] * len(operands)
            + [
                pl.BlockSpec((w_blocks, width), lambda i, info: (0, info[1])),
                pl.BlockSpec((send_rows, width), lambda i, info: (0, 0)),
                pl.BlockSpec((send_rows, width), lambda i, info: (0, 0)),
            ],
            out_specs=pl.BlockSpec((rows, width), lambda i, info: (0, 0)),
        ),
        out_shape=jax.ShapeDtypeStruct((rows, width), jnp.bfloat16),
        compiler_params=pltpu.CompilerParams(vmem_limit_bytes=40 * 2**20),
        cost_estimate=pl.CostEstimate(
            flops=2 * rows * 2 * width * width, bytes_accessed=8 * 2**20, transcendentals=0
        ),
        name="out",
    )(info, *operands, w_out, w_same, w_swap)

    next_head = lax.ppermute(page_head, "ctx", [(i, i - 1) for i in range(1, count)])
    kv_cache = write_pages(keys, values, next_head, index, starts, page_table)
    return attn_out, kv_cache


def write_pages(keys, values, next_head, index, starts, page_table):
    rows, features = keys.shape
    slots = rows // PAGE + 3
    token = index * rows + jnp.arange(rows + PAGE, dtype=jnp.int32)
    exists = token < lax.axis_size("ctx") * rows
    prompt = jnp.sum((starts[None, :] <= token[:, None]).astype(jnp.int32), axis=1) - 1
    position = token - first_of_prompt(token, starts)
    page, offset = position // PAGE, position % PAGE
    owned = exists & ((token - offset) // rows == index)
    pages = page_table.shape[1]
    entry = jnp.take(page_table.reshape(-1), prompt * pages + jnp.clip(page, 0, pages - 1))
    target = jnp.where(owned, entry % slots * PAGE + offset, -1)
    placing = (jnp.arange(slots * PAGE, dtype=jnp.int32)[:, None] == target[None, :]).astype(
        jnp.bfloat16
    )
    sources = jnp.stack(
        [jnp.concatenate([keys, next_head[0]]), jnp.concatenate([values, next_head[1]])], axis=1
    ).reshape(rows + PAGE, 2 * features)
    written = jnp.dot(placing, sources, preferred_element_type=jnp.float32).astype(jnp.bfloat16)
    return written.reshape(slots, PAGE, 2, features)


def passed_along(value, axis, steps):
    count = lax.axis_size(axis)
    first, last = (max(0, -steps), min(count, count - steps))
    return lax.ppermute(value, axis, [(source, source + steps) for source in range(first, last)])


def normalize(inputs, norm_gain, norm_bias):
    average = jnp.sum(inputs, axis=-1, keepdims=True) / inputs.shape[-1]
    centered = inputs - average
    spread = jnp.sum(centered * centered, axis=-1, keepdims=True) / inputs.shape[-1]
    return centered * lax.rsqrt(spread + EPSILON) * norm_gain + norm_bias


def rotary(inputs, positions):
    quarter = inputs.shape[-1] // 4
    halfway = quarter // 2
    exponent = jnp.arange(0, quarter, 2).astype(jnp.float32) / quarter
    inverse = jnp.power(jnp.float32(10000.0), -exponent)
    angles = positions.astype(jnp.float32)[:, None] * inverse[None, :]
    cosine_table = jnp.concatenate([jnp.cos(angles), jnp.cos(angles)], axis=-1)[:, None, :]
    sine_table = jnp.concatenate([jnp.sin(angles), jnp.sin(angles)], axis=-1)[:, None, :]
    leading = inputs[..., :quarter]
    turned = jnp.concatenate([-leading[..., halfway:], leading[..., :halfway]], axis=-1)
    return jnp.concatenate(
        [leading * cosine_table + turned * sine_table, inputs[..., quarter:]], axis=-1
    )


def segment_positions(segment_rows, row_index, starts):
    table_span = starts.shape[0]
    matches = segment_rows[:, None] == jnp.arange(table_span, dtype=jnp.int32)[None, :]
    first_rows = jnp.sum(jnp.where(matches, starts[None, :], 0), axis=1)
    return row_index - first_rows


def attend(carry_state, query_heads, pair_block, key_marks, query_marks, causal):
    running_max, running_sum, running_acc = carry_state
    scores = jnp.einsum(
        "qhd,khd->hqk", query_heads, pair_block[:, 0], preferred_element_type=jnp.float32
    ) / math.sqrt(query_heads.shape[-1])
    visible = query_marks[:, None] == key_marks[None, :]
    if causal:
        row_count = query_heads.shape[0]
        visible = visible & (jnp.arange(row_count)[None, :] <= jnp.arange(row_count)[:, None])
    scores = jnp.where(visible[None], scores, -jnp.inf)
    newest_max = jnp.maximum(running_max, jnp.max(scores, axis=-1))
    rescale = jnp.exp(running_max - newest_max)
    weights = jnp.exp(scores - newest_max[..., None]).astype(jnp.bfloat16)
    weights = lax.optimization_barrier(weights)
    running_sum = running_sum * rescale + jnp.sum(weights.astype(jnp.float32), axis=-1)
    running_acc = running_acc * rescale[..., None] + jnp.einsum(
        "hqk,khd->hqd", weights, pair_block[:, 1], preferred_element_type=jnp.float32
    )
    return (newest_max, running_sum, running_acc)


def visit_block(carry_state, query_heads, query_marks, pair_block, key_marks):
    tail_mark = key_marks[key_marks.shape[0] - 1]
    relevant = tail_mark == query_marks[0]
    return lax.cond(
        relevant,
        lambda current: attend(current, query_heads, pair_block, key_marks, query_marks, False),
        lambda current: current,
        carry_state,
    )


def relay_pairs(hidden_in, ln_gain, ln_bias, w_qkv, w_out, segment_ids, prompt_lengths, page_table):
    token_rows = hidden_in.shape[0]
    model_width = w_out.shape[1]
    local_heads = w_out.shape[0] // HD
    my_index = lax.axis_index("ctx")
    reach = lax.axis_size("ctx") // 2
    whole_rows = lax.all_gather(hidden_in, "tp", axis=1, tiled=True)
    normed = normalize(whole_rows.astype(jnp.float32), ln_gain, ln_bias).astype(jnp.bfloat16)
    projected = jnp.einsum("td,jdh->tjh", normed, w_qkv, preferred_element_type=jnp.float32)
    starts = jnp.cumsum(prompt_lengths) - prompt_lengths
    row_index = my_index * token_rows + jnp.arange(token_rows, dtype=jnp.int32)
    positions = segment_positions(segment_ids, row_index, starts)
    query_heads = rotary(projected[:, 0].reshape(token_rows, local_heads, HD), positions).astype(
        jnp.bfloat16
    )
    key_heads = rotary(projected[:, 1].reshape(token_rows, local_heads, HD), positions).astype(
        jnp.bfloat16
    )
    value_heads = projected[:, 2].reshape(token_rows, local_heads, HD).astype(jnp.bfloat16)
    pair_block = jnp.stack([key_heads, value_heads], axis=1)
    own_marks = segment_ids + 1
    carry_state = (
        jnp.full((local_heads, token_rows), -jnp.inf, jnp.float32),
        jnp.zeros((local_heads, token_rows), jnp.float32),
        jnp.zeros((local_heads, token_rows, HD), jnp.float32),
    )
    carry_state = attend(carry_state, query_heads, pair_block, own_marks, own_marks, True)

    def relay_step(step, state):
        moving_pair, moving_marks, current = state
        moving_pair, moving_marks = passed_along((moving_pair, moving_marks), "ctx", 1)
        current = visit_block(current, query_heads, own_marks, moving_pair, moving_marks)
        return (moving_pair, moving_marks, current)

    carry_state = lax.fori_loop(0, reach, relay_step, (pair_block, own_marks, carry_state))[2]
    running_max, running_sum, running_acc = carry_state
    attended = (running_acc / running_sum[..., None]).astype(jnp.bfloat16)
    partial_value = jnp.einsum(
        "hqd,hde->qe",
        attended,
        w_out.reshape(local_heads, HD, model_width),
        preferred_element_type=jnp.float32,
    )
    attn_out = lax.psum_scatter(
        partial_value.astype(jnp.bfloat16), "tp", scatter_dimension=1, tiled=True
    )
    tail_pair, tail_marks = passed_along((pair_block[:PAGE], own_marks[:PAGE]), "ctx", -1)
    every_pair = jnp.concatenate([pair_block, tail_pair], axis=0)
    every_marks = jnp.concatenate([own_marks, tail_marks], axis=0)
    every_index = my_index * token_rows + jnp.arange(token_rows + PAGE, dtype=jnp.int32)
    every_segment = jnp.maximum(every_marks - 1, 0)
    every_position = segment_positions(every_segment, every_index, starts)
    page_number = every_position // PAGE
    page_offset = every_position % PAGE
    page_owner = (every_index - page_offset) // token_rows
    is_owned = (every_marks > 0) & (page_owner == my_index)
    page_count = page_table.shape[1]
    table_entry = jnp.take(
        page_table.reshape(-1),
        every_segment * page_count + jnp.clip(page_number, 0, page_count - 1),
    )
    kv_slots = token_rows // PAGE + 3
    target = jnp.where(is_owned, table_entry % kv_slots * PAGE + page_offset, -1)
    placing = (jnp.arange(kv_slots * PAGE, dtype=jnp.int32)[:, None] == target[None, :]).astype(
        jnp.bfloat16
    )
    flat_pair = every_pair.reshape(token_rows + PAGE, 2 * local_heads * HD)
    written = jnp.dot(placing, flat_pair, preferred_element_type=jnp.float32).astype(jnp.bfloat16)
    kv_cache = written.reshape(kv_slots, PAGE, 2, local_heads * HD)
    return (attn_out, kv_cache)


def per_device(*operands):
    heads = operands[4].shape[0] // HD
    spread = lax.axis_size("tp") == 2 and lax.axis_size("ctx") == 4 * heads
    return (split_heads if spread else relay_pairs)(*operands)


def solution(mesh):
    return jax.shard_map(
        per_device,
        mesh=mesh,
        in_specs=(P("ctx", "tp"), P(), P(), P(None, None, "tp"), P("tp", None), P("ctx"), P(), P()),
        out_specs=(P("ctx", "tp"), P("ctx", None, None, "tp")),
        check_vma=False,
    )
```

```python
import functools
import math

import jax
import jax.numpy as jnp
from jax import lax
from jax.experimental import pallas as pl
from jax.experimental.pallas import tpu as pltpu
from jax.sharding import PartitionSpec as P

HD = 256
PAGE = 128
EPSILON = 1e-05
ROT = HD // 4
LANES = 128
VMEM = pltpu.VMEM
MASKED = -1e30
LOG2E = 1.4426950408889634


def cost(microseconds):
    return pl.CostEstimate(flops=int(microseconds * 0.35e9), bytes_accessed=0, transcendentals=0)


def row_bounds(info, rows):
    first = jnp.zeros_like(rows)
    for prompt in range(3, 6):
        first = jnp.where(rows >= info[prompt], info[prompt], first)
    return first


def load_kernel(
    splits,
    lengths,
    own,
    gain,
    bias,
    inverse,
    w_qkv,
    w_out,
    info,
    own_here,
    gain_here,
    bias_here,
    keep,
    below,
    above,
    weights,
    own_columns,
    outgoing,
    sems,
):
    index, rank = lax.axis_index("ctx"), lax.axis_index("tp")
    core = lax.rem(index, 2)
    rows, width = own_here.shape
    send_rows = outgoing.shape[0]

    def columns(place):
        return pl.ds(pl.multiple_of(place * width, width), width)

    sent = pl.ds(pl.multiple_of(core * send_rows, send_rows), send_rows)
    pieces = (
        (own, own_here),
        (gain, gain_here),
        (bias, bias_here),
        (w_qkv, weights),
        (w_out.at[sent, columns(1 - rank)], outgoing),
        (w_out.at[:, columns(rank)], own_columns),
    )
    copies = [pltpu.make_async_copy(*piece, sems.at[i]) for i, piece in enumerate(pieces)]
    for copy in copies:
        copy.start()
    info[0] = lax.rem(index // 2, splits)
    info[1] = rank
    info[2] = core
    info[3] = 0
    info[4] = lengths[0]
    info[5] = lengths[0] + lengths[1]
    info[6] = index // (2 * splits) * (2 * splits * rows)
    info[7] = index
    row = index * rows + lax.broadcasted_iota(jnp.int32, (rows, 1), 0)
    position = (row - row_bounds(info, row)).astype(jnp.float32)
    angles = position * inverse[...]
    cosine, sine = jnp.cos(angles), jnp.sin(angles)
    lane = lax.broadcasted_iota(jnp.int32, cosine.shape, 1)
    keep[...] = jnp.where(lane < ROT, cosine, 1.0)
    below[...] = jnp.where((lane >= ROT // 2) & (lane < ROT), sine, 0.0)
    above[...] = jnp.where(lane < ROT // 2, -sine, 0.0)
    for copy in copies:
        copy.wait()


def load(splits, lengths, own, gain, bias, w_qkv, w_out):
    rows, width = own.shape
    exponent = jnp.arange(0, ROT, 2).astype(jnp.float32) / ROT
    inverse = jnp.power(jnp.float32(10000.0), -exponent)
    inverse = jnp.tile(inverse, LANES // (ROT // 2))[None, :]
    smem, here = pl.BlockSpec(memory_space=pltpu.SMEM), pl.BlockSpec(memory_space=pltpu.VMEM)
    table = jax.ShapeDtypeStruct((rows, LANES), jnp.float32)
    wide = jax.ShapeDtypeStruct(gain.shape, jnp.float32)
    narrow = lambda *shape: jax.ShapeDtypeStruct(shape, jnp.bfloat16)
    return pl.pallas_call(
        functools.partial(load_kernel, splits),
        in_specs=[smem] + [pl.BlockSpec(memory_space=pltpu.HBM)] * 3 + [here]
        + [pl.BlockSpec(memory_space=pltpu.HBM)] * 2,
        out_specs=[smem] + [here] * 9,
        out_shape=[
            jax.ShapeDtypeStruct((8,), jnp.int32),
            narrow(rows, width),
            wide,
            wide,
            table,
            table,
            table,
            narrow(*w_qkv.shape),
            narrow(w_out.shape[0], width),
            narrow(w_out.shape[0] // 2, width),
        ],
        scratch_shapes=[pltpu.SemaphoreType.DMA((6,))],
        compiler_params=pltpu.CompilerParams(vmem_limit_bytes=24 * 2**20),
        cost_estimate=cost(6),
        name="load",
    )(lengths, own, gain, bias, inverse, w_qkv, w_out)


def normed_rows(info, own, other, gain, bias, normed):
    width = own.shape[1]
    full = 2 * width
    mine = own[...].astype(jnp.float32)
    theirs = other[...].astype(jnp.float32)
    total = jnp.sum(mine, axis=-1, keepdims=True) + jnp.sum(theirs, axis=-1, keepdims=True)
    average = total / full
    mine, theirs = mine - average, theirs - average
    spread = jnp.sum(mine * mine, axis=-1, keepdims=True) + jnp.sum(
        theirs * theirs, axis=-1, keepdims=True
    )
    scale = lax.rsqrt(spread / full + EPSILON)
    for part, place in ((mine, info[1]), (theirs, 1 - info[1])):
        columns = pl.ds(pl.multiple_of(place * width, width), width)
        normed[:, columns] = (part * scale * gain[:, columns] + bias[:, columns]).astype(
            jnp.bfloat16
        )


def project_head(info, split, normed, keep, below, above, weights, query_ref, pair_ref):
    head = pl.ds(pl.multiple_of((info[0] ^ split) * HD, HD), HD)
    rows = normed[...]

    def turned(inputs):
        leading = inputs[:, :LANES]
        leading = (
            leading * keep[...]
            + pltpu.roll(leading, ROT // 2, 1) * below[...]
            + pltpu.roll(leading, LANES - ROT // 2, 1) * above[...]
        )
        return jnp.concatenate([leading, inputs[:, LANES:]], axis=1).astype(jnp.bfloat16)

    def product(j):
        return jnp.dot(rows, weights[j, :, head], preferred_element_type=jnp.float32)

    pair_ref[:, :HD] = turned(product(1))
    pair_ref[:, HD:] = product(2).astype(jnp.bfloat16)
    query_ref[...] = turned(product(0))


def first_kernel(
    split, info, own, other, gain, bias, keep, below, above, weights, query, pair, normed
):
    normed_rows(info, own, other, gain, bias, normed)
    project_head(info, split, normed, keep, below, above, weights, query, pair)


def next_kernel(split, info, normed, keep, below, above, weights, query, pair):
    project_head(info, split, normed, keep, below, above, weights, query, pair)


def project(info, split, inputs, tables, weights, rows, features):
    is_first = len(inputs) > 1
    here = pl.BlockSpec(memory_space=pltpu.VMEM)
    return pl.pallas_call(
        functools.partial(first_kernel if is_first else next_kernel, split),
        in_specs=[pl.BlockSpec(memory_space=pltpu.SMEM)]
        + [here] * (len(inputs) + len(tables) + 1),
        out_specs=[here] * (2 + is_first),
        out_shape=[
            jax.ShapeDtypeStruct((rows, HD), jnp.bfloat16),
            jax.ShapeDtypeStruct((rows, 2 * HD), jnp.bfloat16),
        ]
        + [jax.ShapeDtypeStruct((rows, features), jnp.bfloat16)] * is_first,
        compiler_params=pltpu.CompilerParams(vmem_limit_bytes=24 * 2**20),
        cost_estimate=cost(2.7 if is_first else 1.7),
        name="project",
    )(info, *inputs, *tables, weights)


def soft_attend(query, keys, values, first_key, last_key, base):
    scores = lax.dot_general(
        query, keys, (((1,), (1,)), ((), ())), preferred_element_type=jnp.float32
    )
    column = base + lax.broadcasted_iota(jnp.int32, scores.shape, 1)
    visible = (column >= first_key) & (column <= last_key)
    scores = jnp.where(visible, scores, MASKED)
    peak = jnp.max(scores, axis=-1, keepdims=True)
    factor = LOG2E / math.sqrt(HD)
    weights = jnp.exp2((scores - peak) * factor).astype(jnp.bfloat16)
    total = jnp.sum(weights.astype(jnp.float32), axis=-1, keepdims=True)
    mixed = jnp.dot(weights, values, preferred_element_type=jnp.float32) / total
    return mixed, peak * factor + jnp.log2(total)


def fetch_pairs(info, mine, theirs, pairs, sems):
    rows = mine[0].shape[0]
    copies = []
    for refs, core in ((mine, info[2]), (theirs, 1 - info[2])):
        for split, ref in enumerate(refs):
            at = pl.ds(pl.multiple_of((2 * (info[0] ^ split) + core) * rows, rows), rows)
            copies.append(pltpu.make_async_copy(ref, pairs.at[at, :], sems.at[len(copies)]))
    for copy in copies:
        copy.start()
    return copies


def tail_kernel(info, *refs):
    splits = (len(refs) - 4) // 2
    query, mine, theirs = refs[0], refs[1 : splits + 1], refs[splits + 1 : 2 * splits + 1]
    out, pairs, sems = refs[2 * splits + 1 :]
    rows = out.shape[0]

    @pl.when((info[6] == 0) & (info[2] == 0))
    def _():
        copies = fetch_pairs(info, mine, theirs, pairs, sems)
        for copy in copies:
            copy.wait()
        group_rows = 2 * splits * rows
        row = group_rows + lax.broadcasted_iota(jnp.int32, (rows, 1), 0)
        first = row_bounds(info, row)
        mixed, level = soft_attend(query[...], pairs[:, :HD], pairs[:, HD:], first, row, 0)
        level = jnp.where(first < group_rows, level, MASKED)
        out[:, :HD] = mixed.astype(jnp.bfloat16)
        lane = lax.broadcasted_iota(jnp.int32, (rows, LANES), 1)
        high = level.astype(jnp.bfloat16).astype(jnp.float32)
        middle = (level - high).astype(jnp.bfloat16).astype(jnp.float32)
        low = level - high - middle
        out[:, HD:] = jnp.where(
            lane == 0, high, jnp.where(lane == 1, middle, jnp.where(lane == 2, low, 0.0))
        ).astype(jnp.bfloat16)


def main_kernel(info, *refs):
    splits = (len(refs) - 6) // 3
    queries, mine, theirs = refs[:splits], refs[splits : 2 * splits], refs[2 * splits : 3 * splits]
    gathered, near_mixed, near_level, pairs, asked, sems = refs[3 * splits :]
    rows = near_mixed.shape[0]
    copies = fetch_pairs(info, mine, theirs, pairs, sems)
    for split in range(splits):
        at = pl.ds(pl.multiple_of((info[0] ^ split) * rows, rows), rows)
        copies.append(
            pltpu.make_async_copy(queries[split], asked.at[at, :], sems.at[len(copies)])
        )
        copies[-1].start()
    for copy in copies:
        copy.wait()
    for place in range(splits):
        reach = (2 * place + 2) * rows
        row = info[6] + (2 * place + info[2]) * rows + lax.broadcasted_iota(jnp.int32, (rows, 1), 0)
        here = slice(place * rows, (place + 1) * rows)
        mixed, level = soft_attend(
            asked[here, :],
            pairs[:reach, :HD],
            pairs[:reach, HD:],
            row_bounds(info, row),
            row,
            info[6],
        )
        gathered[here, :] = mixed.astype(jnp.bfloat16)
        if place == 0:
            near_mixed[...] = mixed
            near_level[...] = jnp.broadcast_to(level, near_level.shape)


def merge_kernel(info, gathered, near_mixed, near_level, far, *outs):
    rows = near_mixed.shape[0]
    group_rows = 2 * len(outs) * rows
    for split, out in enumerate(outs):
        out[...] = gathered[pl.ds(pl.multiple_of((info[0] ^ split) * rows, rows), rows), :]

    @pl.when((info[6] > 0) & (info[2] == 0))
    def _():
        parts = far[:, HD:].astype(jnp.float32)
        far_level = parts[:, :1] + parts[:, 1:2] + parts[:, 2:3]
        level = near_level[:, :1]
        highest = jnp.maximum(level, far_level)
        near_weight, far_weight = jnp.exp2(level - highest), jnp.exp2(far_level - highest)
        mixed = near_mixed[...] * near_weight + far[:, :HD].astype(jnp.float32) * far_weight
        mixed = mixed / (near_weight + far_weight)
        row = group_rows + lax.broadcasted_iota(jnp.int32, (rows, 1), 0)
        mixed = jnp.where(row < info[5], mixed, near_mixed[...]).astype(jnp.bfloat16)
        for split, out in enumerate(outs):

            @pl.when(info[0] == split)
            def _():
                out[...] = mixed


def page_windows(info, lengths, table, firsts, counts, rows, page):
    slots = firsts.shape[0]
    for slot in range(slots):
        firsts[slot] = 0
        counts[slot] = 0
    for prompt in range(table.shape[0]):

        def visit(j, carry):
            slot = table[prompt, j] - info[7] * slots
            left = lengths[prompt] - j * page

            @pl.when((slot >= 0) & (slot < slots) & (left > 0))
            def _():
                firsts[slot] = info[3 + prompt] + j * page - info[7] * rows
                counts[slot] = jnp.minimum(left, page)

            return carry

        lax.fori_loop(0, table.shape[1], visit, 0)


def page_window(source, first, count, page):
    target = lax.broadcasted_iota(jnp.int32, (page, source.shape[0]), 0)
    origin = lax.broadcasted_iota(jnp.int32, (page, source.shape[0]), 1)
    taken = (origin == target + first) & (target < count)
    window = jnp.dot(taken.astype(jnp.bfloat16), source, preferred_element_type=jnp.float32)
    return jnp.stack([window[:, :HD], window[:, HD:]], axis=1).astype(jnp.bfloat16)


def page_kernel(parts, has_written, info, lengths, table, *refs):
    pairs, (out, firsts, counts) = refs[: len(parts)], refs[len(parts) + has_written :]
    step = pl.program_id(0)
    slots, page = out.shape[:2]

    @pl.when(step == 0)
    def _():
        page_windows(info, lengths, table, firsts, counts, pairs[0].shape[0], page)

    for number in range(len(parts)):

        @pl.when(step == number)
        def _():
            for slot in range(slots):
                out[slot] = page_window(pairs[number][...], firsts[slot], counts[slot], page)


def crossing_kernel(info, lengths, table, *refs):
    splits = len(refs) - 7
    pairs, (following, _, out, block, firsts, counts, sem) = refs[:splits], refs[splits:]
    rows, page = pairs[0].shape[0], block.shape[0]
    page_windows(info, lengths, table, firsts, counts, rows, page)
    following_place = (info[7] + 1) // 2 % splits
    for slot in range(out.shape[0]):

        @pl.when(firsts[slot] + counts[slot] > rows)
        def _():
            for split in range(splits):
                beyond = following[info[0] ^ split ^ following_place]
                source = jnp.concatenate([pairs[split][...], beyond], axis=0)
                columns = pl.ds(pl.multiple_of((info[0] ^ split) * HD, HD), HD)
                block[:, :, columns] = page_window(source, firsts[slot], counts[slot], page)
            copy = pltpu.make_async_copy(block, out.at[slot], sem)
            copy.start()
            copy.wait()


def write_pages(info, lengths, table, pairs, parts, *written):
    rows = pairs[0].shape[0]
    slots = rows // PAGE + 3
    return pl.pallas_call(
        functools.partial(page_kernel, parts, len(written)),
        grid_spec=pltpu.PrefetchScalarGridSpec(
            num_scalar_prefetch=3,
            grid=(len(parts),),
            in_specs=[pl.BlockSpec((rows, 2 * HD), lambda m, *_: (0, 0))] * len(parts)
            + [pl.BlockSpec(memory_space=pl.ANY)] * len(written),
            out_specs=pl.BlockSpec(
                (slots, PAGE, 2, HD), lambda m, info, *_: (0, 0, 0, info[0] ^ (m + parts[0]))
            ),
            scratch_shapes=[pltpu.SMEM((slots,), jnp.int32)] * 2,
        ),
        out_shape=jax.ShapeDtypeStruct((slots, PAGE, 2, len(pairs) * HD), jnp.bfloat16),
        input_output_aliases={3 + len(parts): 0} if written else {},
        compiler_params=pltpu.CompilerParams(vmem_limit_bytes=24 * 2**20),
        cost_estimate=cost(1.8 * len(parts)),
        name="pages",
    )(info, lengths, table, *[pairs[part] for part in parts], *written)


def cross_pages(info, lengths, table, pairs, following, written):
    splits = len(pairs)
    slots = written.shape[0]
    smem, here = pl.BlockSpec(memory_space=pltpu.SMEM), pl.BlockSpec(memory_space=pltpu.VMEM)
    anywhere = pl.BlockSpec(memory_space=pl.ANY)
    return pl.pallas_call(
        crossing_kernel,
        in_specs=[smem] * 3 + [here] * (splits + 1) + [anywhere],
        out_specs=anywhere,
        out_shape=jax.ShapeDtypeStruct(written.shape, written.dtype),
        input_output_aliases={splits + 4: 0},
        scratch_shapes=[
            VMEM(written.shape[1:], written.dtype),
            pltpu.SMEM((slots,), jnp.int32),
            pltpu.SMEM((slots,), jnp.int32),
            pltpu.SemaphoreType.DMA,
        ],
        compiler_params=pltpu.CompilerParams(vmem_limit_bytes=24 * 2**20),
        cost_estimate=cost(3),
        name="crossing",
    )(info, lengths, table, *pairs, following, written)


def on_core(kernel, out_shape, scratch, name, microseconds, direct):
    def call(info, *operands):
        return pl.pallas_call(
            kernel,
            grid_spec=pltpu.PrefetchScalarGridSpec(
                num_scalar_prefetch=1,
                grid=(1,),
                in_specs=[
                    pl.BlockSpec(memory_space=pl.ANY)
                    if number in direct
                    else pl.BlockSpec(value.shape, lambda i, info: (0, 0))
                    for number, value in enumerate(operands)
                ],
                out_specs=[pl.BlockSpec(out.shape, lambda i, info: (0, 0)) for out in out_shape],
                scratch_shapes=scratch,
            ),
            out_shape=out_shape,
            compiler_params=pltpu.CompilerParams(vmem_limit_bytes=24 * 2**20),
            cost_estimate=cost(microseconds),
            name=name,
        )(info, *operands)

    return call


def out_kernel(info, *refs):
    splits = (len(refs) - 4) // 2
    mine, theirs = refs[:splits], refs[splits : 2 * splits]
    w_own, w_same, w_swap, out = refs[2 * splits :]
    half = splits // 2
    total = jnp.zeros(out.shape, jnp.float32)
    for split in range(splits):
        head = info[0] ^ split
        at = pl.ds(pl.multiple_of(head * HD, HD), HD)
        total += jnp.dot(mine[split][...], w_own[at, :], preferred_element_type=jnp.float32)
    for split in range(splits):
        head = info[0] ^ split
        at = pl.ds(pl.multiple_of(lax.rem(head, half) * HD, HD), HD)
        same = head // half == info[2]
        weight = jnp.where(same, w_same[at, :], w_swap[at, :])
        total += jnp.dot(theirs[split][...], weight, preferred_element_type=jnp.float32)
    out[...] = total.astype(jnp.bfloat16)


def split_heads(hidden_in, ln_gain, ln_bias, w_qkv, w_out, segment_ids, prompt_lengths, page_table):
    rows, width = hidden_in.shape
    splits = w_out.shape[0] // HD
    count = lax.axis_size("ctx")
    place = lax.axis_index("ctx") // 2 % splits
    group = 2 * splits

    def across(value, ctx_mask, tp_mask=0):
        pairs = []
        for c in range(count):
            for t in range(2):
                pairs.append((2 * c + t, 2 * (c ^ ctx_mask) + (t ^ tp_mask)))
        return lax.ppermute(value, ("ctx", "tp"), pairs)

    other = across(hidden_in, 0, 1)
    info, own, gain, bias, *tables, weights, own_columns, outgoing = load(
        splits, prompt_lengths, hidden_in, ln_gain[None, :], ln_bias[None, :], w_qkv, w_out
    )
    inputs = (own, other, gain, bias)
    queries, pairs = [None] * splits, [None] * splits
    for split in reversed(range(splits)):
        made = project(info, split, inputs, tables, weights, rows, 2 * width)
        queries[split], pairs[split] = made[:2]
        if len(made) > 2:
            inputs = (made[2],)

    def after(value, *others):
        return lax.optimization_barrier((value, *others))[0]

    kv_mine = [pairs[0]] + [None] * (splits - 1)
    q_mine = [queries[0]] + [None] * (splits - 1)
    for split in reversed(range(1, splits)):
        q_mine[split] = across(queries[split], 2 * split)
    for split in reversed(range(1, splits)):
        kv_mine[split] = across(after(pairs[split], pairs[0]), 2 * split)
    w_same = across(after(outgoing, pairs[0]), 0, 1)
    pages = functools.partial(write_pages, info, prompt_lengths, page_table, pairs)
    half_written = pages(range(splits // 2))
    *q_mine[1:], half_written = lax.optimization_barrier((*q_mine[1:], half_written))
    q_first = q_mine[0]
    for split in range(1, splits):
        q_first = jnp.where(place == split, q_mine[split], q_first)
    q_tail = lax.ppermute(q_first, "ctx", [(group + 2 * s, 2 * s) for s in range(splits)])
    *kv_mine[1:], q_tail = lax.optimization_barrier((*kv_mine[1:], q_tail))
    kv_theirs = [across(kv_mine[split], 1) for split in range(splits)]

    keep_pairs = VMEM((group * rows, 2 * HD), jnp.bfloat16)
    block = jax.ShapeDtypeStruct((rows, HD), jnp.bfloat16)
    (tail,) = on_core(
        tail_kernel,
        [jax.ShapeDtypeStruct((rows, HD + LANES), jnp.bfloat16)],
        [keep_pairs, pltpu.SemaphoreType.DMA((group,))],
        "tail",
        2.7,
        range(1, 2 * splits + 1),
    )(info, q_tail, *kv_mine, *kv_theirs)
    far = lax.ppermute(tail, "ctx", [(2 * s, group + 2 * s) for s in range(splits)])
    page_head = jnp.stack([pair[:PAGE] for pair in pairs])
    page_head = after(page_head, tail)
    following = lax.ppermute(page_head, "ctx", [(i, i - 1) for i in range(1, count)])
    gathered, near_mixed, near_level = on_core(
        main_kernel,
        [
            jax.ShapeDtypeStruct((splits * rows, HD), jnp.bfloat16),
            jax.ShapeDtypeStruct((rows, HD), jnp.float32),
            jax.ShapeDtypeStruct((rows, LANES), jnp.float32),
        ],
        [
            keep_pairs,
            VMEM((splits * rows, HD), jnp.bfloat16),
            pltpu.SemaphoreType.DMA((group + splits,)),
        ],
        "main",
        4.8,
        range(3 * splits),
    )(after(info, tail), *q_mine, *kv_mine, *kv_theirs)
    kv_cache = pages(range(splits // 2, splits), after(half_written, gathered, following))
    blocks = on_core(merge_kernel, [block] * splits, [], "merge", 0.6, ())(
        info, gathered, near_mixed, near_level, after(far, kv_cache)
    )
    w_swap = across(after(w_same, blocks[0]), 1)
    beyond = [across(blocks[s], 2 * s, 1) for s in range(splits)]
    kv_cache = cross_pages(
        after(info, blocks[0]), prompt_lengths, page_table, pairs, following, kv_cache
    )
    near = [blocks[0]] + [across(after(blocks[s], kv_cache), 2 * s) for s in range(1, splits)]
    here = pl.BlockSpec(memory_space=pltpu.VMEM)
    operands = [*near, *beyond, own_columns, w_same, w_swap]
    attn_out = pl.pallas_call(
        out_kernel,
        in_specs=[pl.BlockSpec(memory_space=pltpu.SMEM)] + [here] * len(operands),
        out_shape=jax.ShapeDtypeStruct((rows, width), jnp.bfloat16),
        compiler_params=pltpu.CompilerParams(vmem_limit_bytes=24 * 2**20),
        cost_estimate=cost(2.7),
        name="out",
    )(info, *operands)
    return attn_out, kv_cache


def passed_along(value, axis, steps):
    count = lax.axis_size(axis)
    first, last = (max(0, -steps), min(count, count - steps))
    return lax.ppermute(value, axis, [(source, source + steps) for source in range(first, last)])


def normalize(inputs, norm_gain, norm_bias):
    average = jnp.sum(inputs, axis=-1, keepdims=True) / inputs.shape[-1]
    centered = inputs - average
    spread = jnp.sum(centered * centered, axis=-1, keepdims=True) / inputs.shape[-1]
    return centered * lax.rsqrt(spread + EPSILON) * norm_gain + norm_bias


def rotary(inputs, positions):
    quarter = inputs.shape[-1] // 4
    halfway = quarter // 2
    exponent = jnp.arange(0, quarter, 2).astype(jnp.float32) / quarter
    inverse = jnp.power(jnp.float32(10000.0), -exponent)
    angles = positions.astype(jnp.float32)[:, None] * inverse[None, :]
    cosine_table = jnp.concatenate([jnp.cos(angles), jnp.cos(angles)], axis=-1)[:, None, :]
    sine_table = jnp.concatenate([jnp.sin(angles), jnp.sin(angles)], axis=-1)[:, None, :]
    leading = inputs[..., :quarter]
    turned = jnp.concatenate([-leading[..., halfway:], leading[..., :halfway]], axis=-1)
    return jnp.concatenate(
        [leading * cosine_table + turned * sine_table, inputs[..., quarter:]], axis=-1
    )


def segment_positions(segment_rows, row_index, starts):
    table_span = starts.shape[0]
    matches = segment_rows[:, None] == jnp.arange(table_span, dtype=jnp.int32)[None, :]
    first_rows = jnp.sum(jnp.where(matches, starts[None, :], 0), axis=1)
    return row_index - first_rows


def attend(carry_state, query_heads, pair_block, key_marks, query_marks, causal):
    running_max, running_sum, running_acc = carry_state
    scores = jnp.einsum(
        "qhd,khd->hqk", query_heads, pair_block[:, 0], preferred_element_type=jnp.float32
    ) / math.sqrt(query_heads.shape[-1])
    visible = query_marks[:, None] == key_marks[None, :]
    if causal:
        row_count = query_heads.shape[0]
        visible = visible & (jnp.arange(row_count)[None, :] <= jnp.arange(row_count)[:, None])
    scores = jnp.where(visible[None], scores, -jnp.inf)
    newest_max = jnp.maximum(running_max, jnp.max(scores, axis=-1))
    rescale = jnp.exp(running_max - newest_max)
    weights = jnp.exp(scores - newest_max[..., None]).astype(jnp.bfloat16)
    weights = lax.optimization_barrier(weights)
    running_sum = running_sum * rescale + jnp.sum(weights.astype(jnp.float32), axis=-1)
    running_acc = running_acc * rescale[..., None] + jnp.einsum(
        "hqk,khd->hqd", weights, pair_block[:, 1], preferred_element_type=jnp.float32
    )
    return (newest_max, running_sum, running_acc)


def visit_block(carry_state, query_heads, query_marks, pair_block, key_marks):
    tail_mark = key_marks[key_marks.shape[0] - 1]
    relevant = tail_mark == query_marks[0]
    return lax.cond(
        relevant,
        lambda current: attend(current, query_heads, pair_block, key_marks, query_marks, False),
        lambda current: current,
        carry_state,
    )


def relay_pairs(hidden_in, ln_gain, ln_bias, w_qkv, w_out, segment_ids, prompt_lengths, page_table):
    token_rows = hidden_in.shape[0]
    model_width = w_out.shape[1]
    local_heads = w_out.shape[0] // HD
    my_index = lax.axis_index("ctx")
    reach = lax.axis_size("ctx") // 2
    whole_rows = lax.all_gather(hidden_in, "tp", axis=1, tiled=True)
    normed = normalize(whole_rows.astype(jnp.float32), ln_gain, ln_bias).astype(jnp.bfloat16)
    projected = jnp.einsum("td,jdh->tjh", normed, w_qkv, preferred_element_type=jnp.float32)
    starts = jnp.cumsum(prompt_lengths) - prompt_lengths
    row_index = my_index * token_rows + jnp.arange(token_rows, dtype=jnp.int32)
    positions = segment_positions(segment_ids, row_index, starts)
    query_heads = rotary(projected[:, 0].reshape(token_rows, local_heads, HD), positions).astype(
        jnp.bfloat16
    )
    key_heads = rotary(projected[:, 1].reshape(token_rows, local_heads, HD), positions).astype(
        jnp.bfloat16
    )
    value_heads = projected[:, 2].reshape(token_rows, local_heads, HD).astype(jnp.bfloat16)
    pair_block = jnp.stack([key_heads, value_heads], axis=1)
    own_marks = segment_ids + 1
    carry_state = (
        jnp.full((local_heads, token_rows), -jnp.inf, jnp.float32),
        jnp.zeros((local_heads, token_rows), jnp.float32),
        jnp.zeros((local_heads, token_rows, HD), jnp.float32),
    )
    carry_state = attend(carry_state, query_heads, pair_block, own_marks, own_marks, True)

    def relay_step(step, state):
        moving_pair, moving_marks, current = state
        moving_pair, moving_marks = passed_along((moving_pair, moving_marks), "ctx", 1)
        current = visit_block(current, query_heads, own_marks, moving_pair, moving_marks)
        return (moving_pair, moving_marks, current)

    carry_state = lax.fori_loop(0, reach, relay_step, (pair_block, own_marks, carry_state))[2]
    running_max, running_sum, running_acc = carry_state
    attended = (running_acc / running_sum[..., None]).astype(jnp.bfloat16)
    partial_value = jnp.einsum(
        "hqd,hde->qe",
        attended,
        w_out.reshape(local_heads, HD, model_width),
        preferred_element_type=jnp.float32,
    )
    attn_out = lax.psum_scatter(
        partial_value.astype(jnp.bfloat16), "tp", scatter_dimension=1, tiled=True
    )
    tail_pair, tail_marks = passed_along((pair_block[:PAGE], own_marks[:PAGE]), "ctx", -1)
    every_pair = jnp.concatenate([pair_block, tail_pair], axis=0)
    every_marks = jnp.concatenate([own_marks, tail_marks], axis=0)
    every_index = my_index * token_rows + jnp.arange(token_rows + PAGE, dtype=jnp.int32)
    every_segment = jnp.maximum(every_marks - 1, 0)
    every_position = segment_positions(every_segment, every_index, starts)
    page_number = every_position // PAGE
    page_offset = every_position % PAGE
    page_owner = (every_index - page_offset) // token_rows
    is_owned = (every_marks > 0) & (page_owner == my_index)
    page_count = page_table.shape[1]
    table_entry = jnp.take(
        page_table.reshape(-1),
        every_segment * page_count + jnp.clip(page_number, 0, page_count - 1),
    )
    kv_slots = token_rows // PAGE + 3
    target = jnp.where(is_owned, table_entry % kv_slots * PAGE + page_offset, -1)
    placing = (jnp.arange(kv_slots * PAGE, dtype=jnp.int32)[:, None] == target[None, :]).astype(
        jnp.bfloat16
    )
    flat_pair = every_pair.reshape(token_rows + PAGE, 2 * local_heads * HD)
    written = jnp.dot(placing, flat_pair, preferred_element_type=jnp.float32).astype(jnp.bfloat16)
    kv_cache = written.reshape(kv_slots, PAGE, 2, local_heads * HD)
    return (attn_out, kv_cache)


def per_device(*operands):
    heads = operands[4].shape[0] // HD
    spread = lax.axis_size("tp") == 2 and lax.axis_size("ctx") == 4 * heads
    return (split_heads if spread else relay_pairs)(*operands)


def solution(mesh):
    return jax.shard_map(
        per_device,
        mesh=mesh,
        in_specs=(P("ctx", "tp"), P(), P(), P(None, None, "tp"), P("tp", None), P("ctx"), P(), P()),
        out_specs=(P("ctx", "tp"), P("ctx", None, None, "tp")),
        check_vma=False,
    )
```

```python
import functools
import math

import jax
import jax.numpy as jnp
from jax import lax
from jax.experimental import pallas as pl
from jax.experimental.pallas import tpu as pltpu
from jax.sharding import PartitionSpec as P

HD = 256
PAGE = 128
EPSILON = 1e-05
ROT = HD // 4
LANES = 128
VMEM = pltpu.VMEM
MASKED = -1e30
LOG2E = 1.4426950408889634


def cost(microseconds):
    return pl.CostEstimate(flops=int(microseconds * 0.35e9), bytes_accessed=0, transcendentals=0)


def row_bounds(info, rows):
    first = jnp.zeros_like(rows)
    for prompt in range(3, 6):
        first = jnp.where(rows >= info[prompt], info[prompt], first)
    return first


def page_windows(info, lengths, table, rows):
    slots = (info.shape[0] - 8) // 2
    for entry in range(8, 8 + 2 * slots):
        info[entry] = 0
    for prompt in range(table.shape[0]):

        def visit(j, carry):
            slot = table[prompt, j] - info[7] * slots
            left = lengths[prompt] - j * PAGE

            @pl.when((slot >= 0) & (slot < slots) & (left > 0))
            def _():
                info[8 + slot] = info[3 + prompt] + j * PAGE - info[7] * rows
                info[8 + slots + slot] = jnp.minimum(left, PAGE)

            return carry

        lax.fori_loop(0, table.shape[1], visit, 0)


def load_kernel(
    splits,
    lengths,
    table,
    own,
    gain,
    bias,
    inverse,
    w_qkv,
    w_out,
    info,
    own_here,
    gain_here,
    bias_here,
    keep,
    below,
    above,
    weights,
    own_columns,
    outgoing,
    sems,
):
    index, rank = lax.axis_index("ctx"), lax.axis_index("tp")
    core = lax.rem(index, 2)
    rows, width = own_here.shape
    send_rows = outgoing.shape[0]

    def columns(place):
        return pl.ds(pl.multiple_of(place * width, width), width)

    sent = pl.ds(pl.multiple_of(core * send_rows, send_rows), send_rows)
    pieces = (
        (own, own_here),
        (gain, gain_here),
        (bias, bias_here),
        (w_qkv, weights),
        (w_out.at[sent, columns(1 - rank)], outgoing),
        (w_out.at[:, columns(rank)], own_columns),
    )
    copies = [pltpu.make_async_copy(*piece, sems.at[i]) for i, piece in enumerate(pieces)]
    for copy in copies:
        copy.start()
    info[0] = lax.rem(index // 2, splits)
    info[1] = rank
    info[2] = core
    info[3] = 0
    info[4] = lengths[0]
    info[5] = lengths[0] + lengths[1]
    info[6] = index // (2 * splits) * (2 * splits * rows)
    info[7] = index
    page_windows(info, lengths, table, rows)
    row = index * rows + lax.broadcasted_iota(jnp.int32, (rows, 1), 0)
    position = (row - row_bounds(info, row)).astype(jnp.float32)
    angles = position * inverse[...]
    cosine, sine = jnp.cos(angles), jnp.sin(angles)
    lane = lax.broadcasted_iota(jnp.int32, cosine.shape, 1)
    keep[...] = jnp.where(lane < ROT, cosine, 1.0)
    below[...] = jnp.where((lane >= ROT // 2) & (lane < ROT), sine, 0.0)
    above[...] = jnp.where(lane < ROT // 2, -sine, 0.0)
    for copy in copies:
        copy.wait()


def load(splits, lengths, page_table, own, gain, bias, w_qkv, w_out):
    rows, width = own.shape
    exponent = jnp.arange(0, ROT, 2).astype(jnp.float32) / ROT
    inverse = jnp.power(jnp.float32(10000.0), -exponent)
    inverse = jnp.tile(inverse, LANES // (ROT // 2))[None, :]
    smem, here = pl.BlockSpec(memory_space=pltpu.SMEM), pl.BlockSpec(memory_space=pltpu.VMEM)
    rotary = jax.ShapeDtypeStruct((rows, LANES), jnp.float32)
    slots = rows // PAGE + 3
    wide = jax.ShapeDtypeStruct(gain.shape, jnp.float32)
    narrow = lambda *shape: jax.ShapeDtypeStruct(shape, jnp.bfloat16)
    return pl.pallas_call(
        functools.partial(load_kernel, splits),
        in_specs=[smem] * 2 + [pl.BlockSpec(memory_space=pltpu.HBM)] * 3 + [here]
        + [pl.BlockSpec(memory_space=pltpu.HBM)] * 2,
        out_specs=[smem] + [here] * 9,
        out_shape=[
            jax.ShapeDtypeStruct((8 + 2 * slots,), jnp.int32),
            narrow(rows, width),
            wide,
            wide,
            rotary,
            rotary,
            rotary,
            narrow(*w_qkv.shape),
            narrow(w_out.shape[0], width),
            narrow(w_out.shape[0] // 2, width),
        ],
        scratch_shapes=[pltpu.SemaphoreType.DMA((6,))],
        compiler_params=pltpu.CompilerParams(vmem_limit_bytes=24 * 2**20),
        cost_estimate=cost(6),
        name="load",
    )(lengths, page_table, own, gain, bias, inverse, w_qkv, w_out)


def normed_rows(info, own, other, gain, bias, normed):
    width = own.shape[1]
    full = 2 * width
    mine = own[...].astype(jnp.float32)
    theirs = other[...].astype(jnp.float32)
    total = jnp.sum(mine, axis=-1, keepdims=True) + jnp.sum(theirs, axis=-1, keepdims=True)
    average = total / full
    mine, theirs = mine - average, theirs - average
    spread = jnp.sum(mine * mine, axis=-1, keepdims=True) + jnp.sum(
        theirs * theirs, axis=-1, keepdims=True
    )
    scale = lax.rsqrt(spread / full + EPSILON)
    for part, place in ((mine, info[1]), (theirs, 1 - info[1])):
        columns = pl.ds(pl.multiple_of(place * width, width), width)
        normed[:, columns] = (part * scale * gain[:, columns] + bias[:, columns]).astype(
            jnp.bfloat16
        )


def turned(inputs, keep, below, above):
    leading = inputs[:, :LANES]
    leading = (
        leading * keep[...]
        + pltpu.roll(leading, ROT // 2, 1) * below[...]
        + pltpu.roll(leading, LANES - ROT // 2, 1) * above[...]
    )
    return jnp.concatenate([leading, inputs[:, LANES:]], axis=1).astype(jnp.bfloat16)


def query_kernel(info, own, other, gain, bias, keep, below, above, weights, *refs):
    queries, normed = refs[:-1], refs[-1]
    normed_rows(info, own, other, gain, bias, normed)
    rows = normed[...]
    for split in reversed(range(len(queries))):
        head = pl.ds(pl.multiple_of((info[0] ^ split) * HD, HD), HD)
        product = jnp.dot(rows, weights[0, :, head], preferred_element_type=jnp.float32)
        queries[split][...] = turned(product, keep, below, above)


def pair_kernel(info, normed, keep, below, above, weights, *refs):
    pairs, head_ref = refs[:-1], refs[-1]
    rows = normed[...]
    for split in reversed(range(len(pairs))):
        head = pl.ds(pl.multiple_of((info[0] ^ split) * HD, HD), HD)
        key = jnp.dot(rows, weights[1, :, head], preferred_element_type=jnp.float32)
        value = jnp.dot(rows, weights[2, :, head], preferred_element_type=jnp.float32)
        pairs[split][:, :HD] = turned(key, keep, below, above)
        pairs[split][:, HD:] = value.astype(jnp.bfloat16)
        head_ref[split] = pairs[split][:PAGE, :]


def project(kernel, outs, name, microseconds, info, *operands):
    here = pl.BlockSpec(memory_space=pltpu.VMEM)
    return pl.pallas_call(
        kernel,
        in_specs=[pl.BlockSpec(memory_space=pltpu.SMEM)] + [here] * len(operands),
        out_specs=[here] * len(outs),
        out_shape=[jax.ShapeDtypeStruct(shape, jnp.bfloat16) for shape in outs],
        compiler_params=pltpu.CompilerParams(vmem_limit_bytes=16 * 2**20),
        cost_estimate=cost(microseconds),
        name=name,
    )(info, *operands)


def softmax_mix(scores, values):
    peak = functools.reduce(
        jnp.maximum, [jnp.max(part, axis=-1, keepdims=True) for part in scores]
    )
    factor = LOG2E / math.sqrt(HD)
    total, mixed = 0.0, 0.0
    for part, value in zip(scores, values):
        weights = jnp.exp2((part - peak) * factor)
        total += jnp.sum(weights, axis=-1, keepdims=True)
        mixed += jnp.dot(
            weights.astype(jnp.bfloat16), value[...], preferred_element_type=jnp.float32
        )
    return mixed / total, peak * factor + jnp.log2(total)


def score(query, keys):
    return lax.dot_general(
        query, keys, (((1,), (1,)), ((), ())), preferred_element_type=jnp.float32
    )


def soft_attend(query, pairs, reach, bounded, causal, base, first_key, last_key):
    cuts = sorted({0, min(bounded, reach), reach - causal, reach})
    scores, values = [], []
    for low, high in zip(cuts, cuts[1:]):
        part = score(query, pairs[low:high, :HD])
        if low < bounded or high > reach - causal:
            column = base + low + lax.broadcasted_iota(jnp.int32, part.shape, 1)
            visible = column >= first_key if low < bounded else column <= last_key
            if low < bounded and high > reach - causal:
                visible = visible & (column <= last_key)
            part = jnp.where(visible, part, MASKED)
        scores.append(part)
        values.append(pairs.at[low:high, HD:])
    return softmax_mix(scores, values)


def pick_kernel(info, *refs):
    for split, ref in enumerate(refs[:-1]):

        @pl.when(info[0] == split)
        def _():
            refs[-1][...] = ref[...]


def tail_kernel(info, *refs):
    splits = (len(refs) - 2) // 2
    query_ref, out = refs[0], refs[-1]
    mine, theirs = refs[1 : splits + 1], refs[splits + 1 : 2 * splits + 1]
    rows = out.shape[0]

    @pl.when((info[6] == 0) & (info[2] == 0))
    def _():
        query = query_ref[...]
        group_rows = 2 * splits * rows
        row = group_rows + lax.broadcasted_iota(jnp.int32, (rows, 1), 0)
        first = row_bounds(info, row)
        scores = []
        for split in range(splits):
            part = score(query, mine[split][:, :HD])
            column = 2 * (info[0] ^ split) * rows + lax.broadcasted_iota(jnp.int32, part.shape, 1)
            scores.append(jnp.where(column >= first, part, MASKED))
        scores += [score(query, ref[:, :HD]) for ref in theirs]
        mixed, level = softmax_mix(scores, [ref.at[:, HD:] for ref in (*mine, *theirs)])
        level = jnp.where(first < group_rows, level, MASKED)
        out[:, :HD] = mixed.astype(jnp.bfloat16)
        lane = lax.broadcasted_iota(jnp.int32, (rows, LANES), 1)
        high = level.astype(jnp.bfloat16).astype(jnp.float32)
        middle = (level - high).astype(jnp.bfloat16).astype(jnp.float32)
        low = level - high - middle
        out[:, HD:] = jnp.where(
            lane == 0, high, jnp.where(lane == 1, middle, jnp.where(lane == 2, low, 0.0))
        ).astype(jnp.bfloat16)


def main_kernel(info, *refs):
    splits = (len(refs) - 6) // 3
    queries, mine, theirs = refs[:splits], refs[splits : 2 * splits], refs[2 * splits : 3 * splits]
    gathered, near_mixed, near_level, pairs, asked, sems = refs[3 * splits :]
    rows = near_mixed.shape[0]

    def at(block):
        return pl.ds(pl.multiple_of(block * rows, rows), rows)

    def fetch(ref, target, block, sem):
        return pltpu.make_async_copy(ref, target.at[at(block), :], sems.at[sem])

    for split in range(splits):
        place = info[0] ^ split
        fetch(queries[split], asked, place, 2 * splits + place).start()
        for refs_of, core in ((mine, info[2]), (theirs, 1 - info[2])):
            fetch(refs_of[split], pairs, 2 * place + core, 2 * place + core).start()
    for place in range(splits):
        fetch(queries[0], asked, place, 2 * splits + place).wait()
        for block in (2 * place, 2 * place + 1):
            fetch(mine[0], pairs, block, block).wait()
        row = info[6] + (2 * place + info[2]) * rows + lax.broadcasted_iota(jnp.int32, (rows, 1), 0)
        here = slice(place * rows, (place + 1) * rows)
        mixed, level = soft_attend(
            asked[here, :],
            pairs,
            (2 * place + 2) * rows,
            rows,
            2 * rows,
            info[6],
            row_bounds(info, row),
            row,
        )
        gathered[here, :] = mixed.astype(jnp.bfloat16)
        if place == 0:
            near_mixed[...] = mixed
            near_level[...] = jnp.broadcast_to(level, near_level.shape)


def merge_kernel(info, gathered, near_mixed, near_level, far, *outs):
    rows = near_mixed.shape[0]
    group_rows = 2 * len(outs) * rows
    for split, out in enumerate(outs):
        out[...] = gathered[pl.ds(pl.multiple_of((info[0] ^ split) * rows, rows), rows), :]

    @pl.when((info[6] > 0) & (info[2] == 0))
    def _():
        parts = far[:, HD:].astype(jnp.float32)
        far_level = parts[:, :1] + parts[:, 1:2] + parts[:, 2:3]
        level = near_level[:, :1]
        highest = jnp.maximum(level, far_level)
        near_weight, far_weight = jnp.exp2(level - highest), jnp.exp2(far_level - highest)
        mixed = near_mixed[...] * near_weight + far[:, :HD].astype(jnp.float32) * far_weight
        mixed = mixed / (near_weight + far_weight)
        row = group_rows + lax.broadcasted_iota(jnp.int32, (rows, 1), 0)
        mixed = jnp.where(row < info[5], mixed, near_mixed[...]).astype(jnp.bfloat16)
        for split, out in enumerate(outs):

            @pl.when(info[0] == split)
            def _():
                out[...] = mixed


def page_rows(rows, first, count, page):
    target = lax.broadcasted_iota(jnp.int32, (page, rows), 0)
    origin = lax.broadcasted_iota(jnp.int32, (page, rows), 1)
    return ((origin == target + first) & (target < count)).astype(jnp.bfloat16)


def put_window(out, mixed, slot, column, window):
    page = window.shape[0]
    for number, low in enumerate(range(0, HD, LANES)):
        turn = mixed.at[slot, number]
        turn[pl.ds(0, page, stride=2), :] = window[:, low : low + LANES]
        turn[pl.ds(1, page, stride=2), :] = window[:, HD + low : HD + low + LANES]
        out[slot, :, :, pl.ds(column + low, LANES)] = (
            turn[...].astype(jnp.bfloat16).reshape(page, 2, LANES)
        )


def page_kernel(info, *refs):
    splits = len(refs) - 2
    pairs, (out, mixed) = refs[:splits], refs[splits:]
    slots, page = out.shape[:2]
    for number in range(splits):

        @pl.when(pl.program_id(0) == number)
        def _():
            source = pairs[number][...]
            taken = [
                page_rows(source.shape[0], info[8 + slot], info[8 + slots + slot], page)
                for slot in range(slots)
            ]
            windows = jnp.dot(jnp.concatenate(taken), source, preferred_element_type=jnp.float32)
            for slot in range(slots):
                put_window(out, mixed, slot, 0, windows[slot * page : (slot + 1) * page])


def crossing_kernel(info, *refs):
    splits = len(refs) - 6
    pairs, (following, _, out, block, mixed, sem) = refs[:splits], refs[splits:]
    rows, page = pairs[0].shape[0], block.shape[1]
    slots = out.shape[0]
    following_place = (info[7] + 1) // 2 % splits
    for slot in range(slots):
        first, count = info[8 + slot], info[8 + slots + slot]

        @pl.when(first + count > rows)
        def _():
            taken = page_rows(rows + page, first, count, page)
            for split in range(splits):
                beyond = following[info[0] ^ split ^ following_place]
                source = jnp.concatenate([pairs[split][...], beyond], axis=0)
                window = jnp.dot(taken, source, preferred_element_type=jnp.float32)
                put_window(block, mixed, 0, pl.multiple_of((info[0] ^ split) * HD, HD), window)
            copy = pltpu.make_async_copy(block.at[0], out.at[slot], sem)
            copy.start()
            copy.wait()


def write_pages(info, pairs):
    rows = pairs[0].shape[0]
    splits = len(pairs)
    slots = rows // PAGE + 3
    return pl.pallas_call(
        page_kernel,
        grid_spec=pltpu.PrefetchScalarGridSpec(
            num_scalar_prefetch=1,
            grid=(splits,),
            in_specs=[pl.BlockSpec((rows, 2 * HD), lambda m, *_: (0, 0))] * splits,
            out_specs=pl.BlockSpec(
                (slots, PAGE, 2, HD), lambda m, info: (0, 0, 0, info[0] ^ m)
            ),
            scratch_shapes=[VMEM((slots, HD // LANES, 2 * PAGE, LANES), jnp.float32)],
        ),
        out_shape=jax.ShapeDtypeStruct((slots, PAGE, 2, splits * HD), jnp.bfloat16),
        compiler_params=pltpu.CompilerParams(vmem_limit_bytes=16 * 2**20),
        cost_estimate=cost(0.3),
        name="pages",
    )(info, *pairs)


def cross_pages(info, pairs, following, written):
    splits = len(pairs)
    smem, here = pl.BlockSpec(memory_space=pltpu.SMEM), pl.BlockSpec(memory_space=pltpu.VMEM)
    anywhere = pl.BlockSpec(memory_space=pl.ANY)
    return pl.pallas_call(
        crossing_kernel,
        in_specs=[smem] + [here] * (splits + 1) + [anywhere],
        out_specs=anywhere,
        out_shape=jax.ShapeDtypeStruct(written.shape, written.dtype),
        input_output_aliases={splits + 2: 0},
        scratch_shapes=[
            VMEM((1, *written.shape[1:]), written.dtype),
            VMEM((1, HD // LANES, 2 * PAGE, LANES), jnp.float32),
            pltpu.SemaphoreType.DMA,
        ],
        compiler_params=pltpu.CompilerParams(vmem_limit_bytes=16 * 2**20),
        cost_estimate=cost(1.5),
        name="crossing",
    )(info, *pairs, following, written)


def on_core(kernel, out_shape, scratch, name, microseconds, direct):
    def call(info, *operands):
        return pl.pallas_call(
            kernel,
            grid_spec=pltpu.PrefetchScalarGridSpec(
                num_scalar_prefetch=1,
                grid=(1,),
                in_specs=[
                    pl.BlockSpec(memory_space=pl.ANY)
                    if number in direct
                    else pl.BlockSpec(value.shape, lambda i, info: (0, 0))
                    for number, value in enumerate(operands)
                ],
                out_specs=[pl.BlockSpec(out.shape, lambda i, info: (0, 0)) for out in out_shape],
                scratch_shapes=scratch,
            ),
            out_shape=out_shape,
            compiler_params=pltpu.CompilerParams(vmem_limit_bytes=16 * 2**20),
            cost_estimate=cost(microseconds),
            name=name,
        )(info, *operands)

    return call


def out_own_kernel(info, *refs):
    splits = len(refs) - 2
    blocks, (w_own, out) = refs[:splits], refs[splits:]
    total = jnp.zeros(out.shape, jnp.float32)
    for split in range(splits):
        at = pl.ds(pl.multiple_of((info[0] ^ split) * HD, HD), HD)
        total += jnp.dot(blocks[split][...], w_own[at, :], preferred_element_type=jnp.float32)
    out[...] = total


def out_theirs_kernel(info, *refs):
    splits = len(refs) - 4
    blocks, (w_same, w_swap, ours, out) = refs[:splits], refs[splits:]
    half = splits // 2
    total = ours[...]
    for weight, core in ((w_same, info[2]), (w_swap, 1 - info[2])):
        for number in range(half):
            split = info[0] ^ (core * half + number)
            block = blocks[0][...]
            for other in range(1, splits):
                block = jnp.where(split == other, blocks[other][...], block)
            total += jnp.dot(
                block,
                weight[number * HD : (number + 1) * HD, :],
                preferred_element_type=jnp.float32,
            )
    out[...] = total.astype(jnp.bfloat16)


def on_chip(kernel, out, name, microseconds):
    here = pl.BlockSpec(memory_space=pltpu.VMEM)
    return lambda info, *operands: pl.pallas_call(
        kernel,
        in_specs=[pl.BlockSpec(memory_space=pltpu.SMEM)] + [here] * len(operands),
        out_specs=here,
        out_shape=out,
        compiler_params=pltpu.CompilerParams(vmem_limit_bytes=16 * 2**20),
        cost_estimate=cost(microseconds),
        name=name,
    )(info, *operands)


def split_heads(hidden_in, ln_gain, ln_bias, w_qkv, w_out, segment_ids, prompt_lengths, page_table):
    rows, width = hidden_in.shape
    splits = w_out.shape[0] // HD
    count = lax.axis_size("ctx")
    group = 2 * splits

    def across(value, ctx_mask, tp_mask=0):
        pairs = []
        for c in range(count):
            for t in range(2):
                pairs.append((2 * c + t, 2 * (c ^ ctx_mask) + (t ^ tp_mask)))
        return lax.ppermute(value, ("ctx", "tp"), pairs)

    other = across(hidden_in, 0, 1)
    info, own, gain, bias, *tables, weights, own_columns, outgoing = load(
        splits, prompt_lengths, page_table, hidden_in, ln_gain[None, :], ln_bias[None, :], w_qkv, w_out
    )
    *queries, normed = project(
        query_kernel,
        [(rows, HD)] * splits + [(rows, 2 * width)],
        "queries",
        3.5,
        info,
        own,
        other,
        gain,
        bias,
        *tables,
        weights,
    )
    *pairs, page_head = project(
        pair_kernel,
        [(rows, 2 * HD)] * splits + [(splits, PAGE, 2 * HD)],
        "pairs",
        6,
        info,
        normed,
        *tables,
        weights,
    )

    def after(value, *others):
        return lax.optimization_barrier((value, *others))[0]

    kv_mine = [pairs[0]] + [None] * (splits - 1)
    q_mine = [queries[0]] + [None] * (splits - 1)
    for split in reversed(range(1, splits)):
        q_mine[split] = across(queries[split], 2 * split)
    for split in reversed(range(1, splits)):
        kv_mine[split] = across(pairs[split], 2 * split)
    q_first = on_chip(pick_kernel, jax.ShapeDtypeStruct((rows, HD), jnp.bfloat16), "pick", 0.3)(
        info, *q_mine
    )
    q_tail = lax.ppermute(q_first, "ctx", [(group + 2 * s, 2 * s) for s in range(splits)])
    kv_cache = write_pages(after(info, q_first), pairs)
    *kv_mine[1:], q_tail, kv_cache = lax.optimization_barrier((*kv_mine[1:], q_tail, kv_cache))
    kv_theirs = [across(kv_mine[split], 1) for split in range(splits)]
    w_same = across(after(outgoing, normed), 0, 1)

    tail = on_chip(
        tail_kernel, jax.ShapeDtypeStruct((rows, HD + LANES), jnp.bfloat16), "tail", 2.7
    )(after(info, kv_cache), q_tail, *kv_mine, *kv_theirs)
    w_swap = across(after(w_same, tail), 1)
    far = lax.ppermute(tail, "ctx", [(2 * s, group + 2 * s) for s in range(splits)])
    page_head = after(page_head, tail)
    following = lax.ppermute(page_head, "ctx", [(i, i - 1) for i in range(1, count)])
    gathered, near_mixed, near_level = on_core(
        main_kernel,
        [
            jax.ShapeDtypeStruct((splits * rows, HD), jnp.bfloat16),
            jax.ShapeDtypeStruct((rows, HD), jnp.float32),
            jax.ShapeDtypeStruct((rows, LANES), jnp.float32),
        ],
        [
            VMEM((group * rows, 2 * HD), jnp.bfloat16),
            VMEM((splits * rows, HD), jnp.bfloat16),
            pltpu.SemaphoreType.DMA((group + splits,)),
        ],
        "main",
        4.8,
        range(3 * splits),
    )(after(info, tail), *q_mine, *kv_mine, *kv_theirs)
    block = jax.ShapeDtypeStruct((rows, HD), jnp.bfloat16)
    blocks = on_core(merge_kernel, [block] * splits, [], "merge", 0.6, ())(
        after(info, w_swap), gathered, near_mixed, near_level, far
    )
    near = [blocks[0]] + [across(blocks[s], 2 * s) for s in range(1, splits)]
    beyond = [across(blocks[s], 2 * s, 1) for s in range(splits)]
    kv_cache = cross_pages(after(info, blocks[0]), pairs, following, kv_cache)
    ours = on_chip(
        out_own_kernel, jax.ShapeDtypeStruct((rows, width), jnp.float32), "out_own", 1.4
    )(info, *near, own_columns)
    attn_out = on_chip(
        out_theirs_kernel, jax.ShapeDtypeStruct((rows, width), jnp.bfloat16), "out_theirs", 2
    )(info, *beyond, w_same, w_swap, ours)
    return attn_out, kv_cache


def passed_along(value, axis, steps):
    count = lax.axis_size(axis)
    first, last = (max(0, -steps), min(count, count - steps))
    return lax.ppermute(value, axis, [(source, source + steps) for source in range(first, last)])


def normalize(inputs, norm_gain, norm_bias):
    average = jnp.sum(inputs, axis=-1, keepdims=True) / inputs.shape[-1]
    centered = inputs - average
    spread = jnp.sum(centered * centered, axis=-1, keepdims=True) / inputs.shape[-1]
    return centered * lax.rsqrt(spread + EPSILON) * norm_gain + norm_bias


def rotary(inputs, positions):
    quarter = inputs.shape[-1] // 4
    halfway = quarter // 2
    exponent = jnp.arange(0, quarter, 2).astype(jnp.float32) / quarter
    inverse = jnp.power(jnp.float32(10000.0), -exponent)
    angles = positions.astype(jnp.float32)[:, None] * inverse[None, :]
    cosine_table = jnp.concatenate([jnp.cos(angles), jnp.cos(angles)], axis=-1)[:, None, :]
    sine_table = jnp.concatenate([jnp.sin(angles), jnp.sin(angles)], axis=-1)[:, None, :]
    leading = inputs[..., :quarter]
    turned = jnp.concatenate([-leading[..., halfway:], leading[..., :halfway]], axis=-1)
    return jnp.concatenate(
        [leading * cosine_table + turned * sine_table, inputs[..., quarter:]], axis=-1
    )


def segment_positions(segment_rows, row_index, starts):
    table_span = starts.shape[0]
    matches = segment_rows[:, None] == jnp.arange(table_span, dtype=jnp.int32)[None, :]
    first_rows = jnp.sum(jnp.where(matches, starts[None, :], 0), axis=1)
    return row_index - first_rows


def attend(carry_state, query_heads, pair_block, key_marks, query_marks, causal):
    running_max, running_sum, running_acc = carry_state
    scores = jnp.einsum(
        "qhd,khd->hqk", query_heads, pair_block[:, 0], preferred_element_type=jnp.float32
    ) / math.sqrt(query_heads.shape[-1])
    visible = query_marks[:, None] == key_marks[None, :]
    if causal:
        row_count = query_heads.shape[0]
        visible = visible & (jnp.arange(row_count)[None, :] <= jnp.arange(row_count)[:, None])
    scores = jnp.where(visible[None], scores, -jnp.inf)
    newest_max = jnp.maximum(running_max, jnp.max(scores, axis=-1))
    rescale = jnp.exp(running_max - newest_max)
    weights = jnp.exp(scores - newest_max[..., None]).astype(jnp.bfloat16)
    weights = lax.optimization_barrier(weights)
    running_sum = running_sum * rescale + jnp.sum(weights.astype(jnp.float32), axis=-1)
    running_acc = running_acc * rescale[..., None] + jnp.einsum(
        "hqk,khd->hqd", weights, pair_block[:, 1], preferred_element_type=jnp.float32
    )
    return (newest_max, running_sum, running_acc)


def visit_block(carry_state, query_heads, query_marks, pair_block, key_marks):
    tail_mark = key_marks[key_marks.shape[0] - 1]
    relevant = tail_mark == query_marks[0]
    return lax.cond(
        relevant,
        lambda current: attend(current, query_heads, pair_block, key_marks, query_marks, False),
        lambda current: current,
        carry_state,
    )


def relay_pairs(hidden_in, ln_gain, ln_bias, w_qkv, w_out, segment_ids, prompt_lengths, page_table):
    token_rows = hidden_in.shape[0]
    model_width = w_out.shape[1]
    local_heads = w_out.shape[0] // HD
    my_index = lax.axis_index("ctx")
    reach = lax.axis_size("ctx") // 2
    whole_rows = lax.all_gather(hidden_in, "tp", axis=1, tiled=True)
    normed = normalize(whole_rows.astype(jnp.float32), ln_gain, ln_bias).astype(jnp.bfloat16)
    projected = jnp.einsum("td,jdh->tjh", normed, w_qkv, preferred_element_type=jnp.float32)
    starts = jnp.cumsum(prompt_lengths) - prompt_lengths
    row_index = my_index * token_rows + jnp.arange(token_rows, dtype=jnp.int32)
    positions = segment_positions(segment_ids, row_index, starts)
    query_heads = rotary(projected[:, 0].reshape(token_rows, local_heads, HD), positions).astype(
        jnp.bfloat16
    )
    key_heads = rotary(projected[:, 1].reshape(token_rows, local_heads, HD), positions).astype(
        jnp.bfloat16
    )
    value_heads = projected[:, 2].reshape(token_rows, local_heads, HD).astype(jnp.bfloat16)
    pair_block = jnp.stack([key_heads, value_heads], axis=1)
    own_marks = segment_ids + 1
    carry_state = (
        jnp.full((local_heads, token_rows), -jnp.inf, jnp.float32),
        jnp.zeros((local_heads, token_rows), jnp.float32),
        jnp.zeros((local_heads, token_rows, HD), jnp.float32),
    )
    carry_state = attend(carry_state, query_heads, pair_block, own_marks, own_marks, True)

    def relay_step(step, state):
        moving_pair, moving_marks, current = state
        moving_pair, moving_marks = passed_along((moving_pair, moving_marks), "ctx", 1)
        current = visit_block(current, query_heads, own_marks, moving_pair, moving_marks)
        return (moving_pair, moving_marks, current)

    carry_state = lax.fori_loop(0, reach, relay_step, (pair_block, own_marks, carry_state))[2]
    running_max, running_sum, running_acc = carry_state
    attended = (running_acc / running_sum[..., None]).astype(jnp.bfloat16)
    partial_value = jnp.einsum(
        "hqd,hde->qe",
        attended,
        w_out.reshape(local_heads, HD, model_width),
        preferred_element_type=jnp.float32,
    )
    attn_out = lax.psum_scatter(
        partial_value.astype(jnp.bfloat16), "tp", scatter_dimension=1, tiled=True
    )
    tail_pair, tail_marks = passed_along((pair_block[:PAGE], own_marks[:PAGE]), "ctx", -1)
    every_pair = jnp.concatenate([pair_block, tail_pair], axis=0)
    every_marks = jnp.concatenate([own_marks, tail_marks], axis=0)
    every_index = my_index * token_rows + jnp.arange(token_rows + PAGE, dtype=jnp.int32)
    every_segment = jnp.maximum(every_marks - 1, 0)
    every_position = segment_positions(every_segment, every_index, starts)
    page_number = every_position // PAGE
    page_offset = every_position % PAGE
    page_owner = (every_index - page_offset) // token_rows
    is_owned = (every_marks > 0) & (page_owner == my_index)
    page_count = page_table.shape[1]
    table_entry = jnp.take(
        page_table.reshape(-1),
        every_segment * page_count + jnp.clip(page_number, 0, page_count - 1),
    )
    kv_slots = token_rows // PAGE + 3
    target = jnp.where(is_owned, table_entry % kv_slots * PAGE + page_offset, -1)
    placing = (jnp.arange(kv_slots * PAGE, dtype=jnp.int32)[:, None] == target[None, :]).astype(
        jnp.bfloat16
    )
    flat_pair = every_pair.reshape(token_rows + PAGE, 2 * local_heads * HD)
    written = jnp.dot(placing, flat_pair, preferred_element_type=jnp.float32).astype(jnp.bfloat16)
    kv_cache = written.reshape(kv_slots, PAGE, 2, local_heads * HD)
    return (attn_out, kv_cache)


def per_device(*operands):
    heads = operands[4].shape[0] // HD
    spread = lax.axis_size("tp") == 2 and lax.axis_size("ctx") == 4 * heads
    return (split_heads if spread else relay_pairs)(*operands)


def solution(mesh):
    return jax.shard_map(
        per_device,
        mesh=mesh,
        in_specs=(P("ctx", "tp"), P(), P(), P(None, None, "tp"), P("tp", None), P("ctx"), P(), P()),
        out_specs=(P("ctx", "tp"), P("ctx", None, None, "tp")),
        check_vma=False,
    )
```

```python
import functools
import math

import jax
import jax.numpy as jnp
from jax import lax
from jax.experimental import pallas as pl
from jax.experimental.pallas import tpu as pltpu
from jax.sharding import PartitionSpec as P

HD = 256
PAGE = 128
EPSILON = 1e-05
ROT = HD // 4
LANES = 128
VMEM = pltpu.VMEM
MASKED = -1e30
LOG2E = 1.4426950408889634


def cost(microseconds):
    return pl.CostEstimate(flops=int(microseconds * 0.35e9), bytes_accessed=0, transcendentals=0)


def row_bounds(info, rows):
    first = jnp.zeros_like(rows)
    for prompt in range(3, 6):
        first = jnp.where(rows >= info[prompt], info[prompt], first)
    return first


def page_windows(info, lengths, table, rows):
    slots = (info.shape[0] - 8) // 2
    for entry in range(8, 8 + 2 * slots):
        info[entry] = 0
    for prompt in range(table.shape[0]):

        def visit(j, carry):
            slot = table[prompt, j] - info[7] * slots
            left = lengths[prompt] - j * PAGE

            @pl.when((slot >= 0) & (slot < slots) & (left > 0))
            def _():
                info[8 + slot] = info[3 + prompt] + j * PAGE - info[7] * rows
                info[8 + slots + slot] = jnp.minimum(left, PAGE)

            return carry

        lax.fori_loop(0, table.shape[1], visit, 0)


def load_kernel(
    splits,
    lengths,
    table,
    own,
    gain,
    bias,
    inverse,
    w_qkv,
    w_out,
    info,
    own_here,
    gain_here,
    bias_here,
    keep,
    below,
    above,
    weights,
    own_columns,
    outgoing,
    sems,
):
    index, rank = lax.axis_index("ctx"), lax.axis_index("tp")
    core = lax.rem(index, 2)
    rows, width = own_here.shape
    send_rows = outgoing.shape[0]

    def columns(place):
        return pl.ds(pl.multiple_of(place * width, width), width)

    sent = pl.ds(pl.multiple_of(core * send_rows, send_rows), send_rows)
    pieces = (
        (own, own_here),
        (gain, gain_here),
        (bias, bias_here),
        (w_qkv, weights),
        (w_out.at[sent, columns(1 - rank)], outgoing),
        (w_out.at[:, columns(rank)], own_columns),
    )
    copies = [pltpu.make_async_copy(*piece, sems.at[i]) for i, piece in enumerate(pieces)]
    for copy in copies:
        copy.start()
    info[0] = lax.rem(index // 2, splits)
    info[1] = rank
    info[2] = core
    info[3] = 0
    info[4] = lengths[0]
    info[5] = lengths[0] + lengths[1]
    info[6] = index // (2 * splits) * (2 * splits * rows)
    info[7] = index
    page_windows(info, lengths, table, rows)
    row = index * rows + lax.broadcasted_iota(jnp.int32, (rows, 1), 0)
    position = (row - row_bounds(info, row)).astype(jnp.float32)
    angles = position * inverse[...]
    cosine, sine = jnp.cos(angles), jnp.sin(angles)
    lane = lax.broadcasted_iota(jnp.int32, cosine.shape, 1)
    keep[...] = jnp.where(lane < ROT, cosine, 1.0)
    below[...] = jnp.where((lane >= ROT // 2) & (lane < ROT), sine, 0.0)
    above[...] = jnp.where(lane < ROT // 2, -sine, 0.0)
    for copy in copies:
        copy.wait()


def load(splits, lengths, page_table, own, gain, bias, w_qkv, w_out):
    rows, width = own.shape
    exponent = jnp.arange(0, ROT, 2).astype(jnp.float32) / ROT
    inverse = jnp.power(jnp.float32(10000.0), -exponent)
    inverse = jnp.tile(inverse, LANES // (ROT // 2))[None, :]
    smem, here = pl.BlockSpec(memory_space=pltpu.SMEM), pl.BlockSpec(memory_space=pltpu.VMEM)
    rotary = jax.ShapeDtypeStruct((rows, LANES), jnp.float32)
    slots = rows // PAGE + 3
    wide = jax.ShapeDtypeStruct(gain.shape, jnp.float32)
    narrow = lambda *shape: jax.ShapeDtypeStruct(shape, jnp.bfloat16)
    return pl.pallas_call(
        functools.partial(load_kernel, splits),
        in_specs=[smem] * 2 + [pl.BlockSpec(memory_space=pltpu.HBM)] * 3 + [here]
        + [pl.BlockSpec(memory_space=pltpu.HBM)] * 2,
        out_specs=[smem] + [here] * 9,
        out_shape=[
            jax.ShapeDtypeStruct((8 + 2 * slots,), jnp.int32),
            narrow(rows, width),
            wide,
            wide,
            rotary,
            rotary,
            rotary,
            narrow(*w_qkv.shape),
            narrow(w_out.shape[0], width),
            narrow(w_out.shape[0] // 2, width),
        ],
        scratch_shapes=[pltpu.SemaphoreType.DMA((6,))],
        compiler_params=pltpu.CompilerParams(vmem_limit_bytes=24 * 2**20),
        cost_estimate=cost(6),
        name="load",
    )(lengths, page_table, own, gain, bias, inverse, w_qkv, w_out)


def normed_rows(info, own, other, gain, bias, normed):
    width = own.shape[1]
    full = 2 * width
    mine = own[...].astype(jnp.float32)
    theirs = other[...].astype(jnp.float32)
    total = jnp.sum(mine, axis=-1, keepdims=True) + jnp.sum(theirs, axis=-1, keepdims=True)
    average = total / full
    mine, theirs = mine - average, theirs - average
    spread = jnp.sum(mine * mine, axis=-1, keepdims=True) + jnp.sum(
        theirs * theirs, axis=-1, keepdims=True
    )
    scale = lax.rsqrt(spread / full + EPSILON)
    for part, place in ((mine, info[1]), (theirs, 1 - info[1])):
        columns = pl.ds(pl.multiple_of(place * width, width), width)
        normed[:, columns] = (part * scale * gain[:, columns] + bias[:, columns]).astype(
            jnp.bfloat16
        )


def turned(inputs, keep, below, above):
    leading = inputs[:, :LANES]
    leading = (
        leading * keep[...]
        + pltpu.roll(leading, ROT // 2, 1) * below[...]
        + pltpu.roll(leading, LANES - ROT // 2, 1) * above[...]
    )
    return jnp.concatenate([leading, inputs[:, LANES:]], axis=1).astype(jnp.bfloat16)


def query_kernel(info, own, other, gain, bias, keep, below, above, weights, *refs):
    queries, normed = refs[:-1], refs[-1]
    normed_rows(info, own, other, gain, bias, normed)
    rows = normed[...]
    for split in reversed(range(len(queries))):
        head = pl.ds(pl.multiple_of((info[0] ^ split) * HD, HD), HD)
        product = jnp.dot(rows, weights[0, :, head], preferred_element_type=jnp.float32)
        queries[split][...] = turned(product, keep, below, above)


def pair_kernel(info, normed, keep, below, above, weights, *refs):
    pairs, head_ref = refs[:-1], refs[-1]
    rows = normed[...]
    for split in reversed(range(len(pairs))):
        head = pl.ds(pl.multiple_of((info[0] ^ split) * HD, HD), HD)
        key = jnp.dot(rows, weights[1, :, head], preferred_element_type=jnp.float32)
        value = jnp.dot(rows, weights[2, :, head], preferred_element_type=jnp.float32)
        pairs[split][:, :HD] = turned(key, keep, below, above)
        pairs[split][:, HD:] = value.astype(jnp.bfloat16)
        head_ref[split] = pairs[split][:PAGE, :]


def project(kernel, outs, name, microseconds, info, *operands):
    here = pl.BlockSpec(memory_space=pltpu.VMEM)
    return pl.pallas_call(
        kernel,
        in_specs=[pl.BlockSpec(memory_space=pltpu.SMEM)] + [here] * len(operands),
        out_specs=[here] * len(outs),
        out_shape=[jax.ShapeDtypeStruct(shape, jnp.bfloat16) for shape in outs],
        compiler_params=pltpu.CompilerParams(vmem_limit_bytes=16 * 2**20),
        cost_estimate=cost(microseconds),
        name=name,
    )(info, *operands)


def softmax_mix(scores, values):
    peak = functools.reduce(
        jnp.maximum, [jnp.max(part, axis=-1, keepdims=True) for part in scores]
    )
    factor = LOG2E / math.sqrt(HD)
    total, mixed = 0.0, 0.0
    for part, value in zip(scores, values):
        weights = jnp.exp2((part - peak) * factor)
        total += jnp.sum(weights, axis=-1, keepdims=True)
        mixed += jnp.dot(
            weights.astype(jnp.bfloat16), value[...], preferred_element_type=jnp.float32
        )
    return mixed / total, peak * factor + jnp.log2(total)


def score(query, keys):
    return lax.dot_general(
        query, keys, (((1,), (1,)), ((), ())), preferred_element_type=jnp.float32
    )


def soft_attend(query, pairs, reach, bounded, causal, base, first_key, last_key):
    cuts = sorted({0, min(bounded, reach), reach - causal, reach})
    scores, values = [], []
    for low, high in zip(cuts, cuts[1:]):
        part = score(query, pairs[low:high, :HD])
        if low < bounded or high > reach - causal:
            column = base + low + lax.broadcasted_iota(jnp.int32, part.shape, 1)
            visible = column >= first_key if low < bounded else column <= last_key
            if low < bounded and high > reach - causal:
                visible = visible & (column <= last_key)
            part = jnp.where(visible, part, MASKED)
        scores.append(part)
        values.append(pairs.at[low:high, HD:])
    return softmax_mix(scores, values)


def pick_kernel(info, *refs):
    for split, ref in enumerate(refs[:-1]):

        @pl.when(info[0] == split)
        def _():
            refs[-1][...] = ref[...]


def tail_kernel(info, *refs):
    splits = (len(refs) - 2) // 2
    query_ref, out = refs[0], refs[-1]
    mine, theirs = refs[1 : splits + 1], refs[splits + 1 : 2 * splits + 1]
    rows = out.shape[0]

    @pl.when((info[6] == 0) & (info[2] == 0))
    def _():
        query = query_ref[...]
        group_rows = 2 * splits * rows
        row = group_rows + lax.broadcasted_iota(jnp.int32, (rows, 1), 0)
        first = row_bounds(info, row)
        scores = []
        for split in range(splits):
            part = score(query, mine[split][:, :HD])
            column = 2 * (info[0] ^ split) * rows + lax.broadcasted_iota(jnp.int32, part.shape, 1)
            scores.append(jnp.where(column >= first, part, MASKED))
        scores += [score(query, ref[:, :HD]) for ref in theirs]
        mixed, level = softmax_mix(scores, [ref.at[:, HD:] for ref in (*mine, *theirs)])
        level = jnp.where(first < group_rows, level, MASKED)
        out[:, :HD] = mixed.astype(jnp.bfloat16)
        lane = lax.broadcasted_iota(jnp.int32, (rows, LANES), 1)
        high = level.astype(jnp.bfloat16).astype(jnp.float32)
        middle = (level - high).astype(jnp.bfloat16).astype(jnp.float32)
        low = level - high - middle
        out[:, HD:] = jnp.where(
            lane == 0, high, jnp.where(lane == 1, middle, jnp.where(lane == 2, low, 0.0))
        ).astype(jnp.bfloat16)


def main_kernel(info, *refs):
    splits = (len(refs) - 5) // 3
    queries, mine, theirs = refs[:splits], refs[splits : 2 * splits], refs[2 * splits : 3 * splits]
    gathered, near_mixed, near_level, pairs, asked = refs[3 * splits :]
    rows = near_mixed.shape[0]

    def at(block):
        return pl.ds(pl.multiple_of(block * rows, rows), rows)

    for split in range(splits):
        place = info[0] ^ split
        asked[at(place), :] = queries[split][...]
        for refs_of, core in ((mine, info[2]), (theirs, 1 - info[2])):
            pairs[at(2 * place + core), :] = refs_of[split][...]
    for place in range(splits):
        row = info[6] + (2 * place + info[2]) * rows + lax.broadcasted_iota(jnp.int32, (rows, 1), 0)
        here = slice(place * rows, (place + 1) * rows)
        mixed, level = soft_attend(
            asked[here, :],
            pairs,
            (2 * place + 2) * rows,
            rows,
            2 * rows,
            info[6],
            row_bounds(info, row),
            row,
        )
        gathered[here, :] = mixed.astype(jnp.bfloat16)
        if place == 0:
            near_mixed[...] = mixed
            near_level[...] = jnp.broadcast_to(level, near_level.shape)


def merge_kernel(info, gathered, near_mixed, near_level, far, *outs):
    rows = near_mixed.shape[0]
    group_rows = 2 * len(outs) * rows
    for split, out in enumerate(outs):
        out[...] = gathered[pl.ds(pl.multiple_of((info[0] ^ split) * rows, rows), rows), :]

    @pl.when((info[6] > 0) & (info[2] == 0))
    def _():
        parts = far[:, HD:].astype(jnp.float32)
        far_level = parts[:, :1] + parts[:, 1:2] + parts[:, 2:3]
        level = near_level[:, :1]
        highest = jnp.maximum(level, far_level)
        near_weight, far_weight = jnp.exp2(level - highest), jnp.exp2(far_level - highest)
        mixed = near_mixed[...] * near_weight + far[:, :HD].astype(jnp.float32) * far_weight
        mixed = mixed / (near_weight + far_weight)
        row = group_rows + lax.broadcasted_iota(jnp.int32, (rows, 1), 0)
        mixed = jnp.where(row < info[5], mixed, near_mixed[...]).astype(jnp.bfloat16)
        for split, out in enumerate(outs):

            @pl.when(info[0] == split)
            def _():
                out[...] = mixed


def page_rows(rows, first, count, page):
    target = lax.broadcasted_iota(jnp.int32, (page, rows), 0)
    origin = lax.broadcasted_iota(jnp.int32, (page, rows), 1)
    return ((origin == target + first) & (target < count)).astype(jnp.bfloat16)


def put_window(out, mixed, slot, column, window):
    page = window.shape[0]
    for number, low in enumerate(range(0, HD, LANES)):
        turn = mixed.at[slot, number]
        turn[pl.ds(0, page, stride=2), :] = window[:, low : low + LANES]
        turn[pl.ds(1, page, stride=2), :] = window[:, HD + low : HD + low + LANES]
        out[slot, :, :, pl.ds(column + low, LANES)] = (
            turn[...].astype(jnp.bfloat16).reshape(page, 2, LANES)
        )


def page_kernel(info, *refs):
    splits = len(refs) - 2
    pairs, (out, mixed) = refs[:splits], refs[splits:]
    slots, page = out.shape[:2]
    for number in range(splits):

        @pl.when(pl.program_id(0) == number)
        def _():
            source = pairs[number][...]
            taken = [
                page_rows(source.shape[0], info[8 + slot], info[8 + slots + slot], page)
                for slot in range(slots)
            ]
            windows = jnp.dot(jnp.concatenate(taken), source, preferred_element_type=jnp.float32)
            for slot in range(slots):
                put_window(out, mixed, slot, 0, windows[slot * page : (slot + 1) * page])


def crossing_kernel(info, *refs):
    splits = len(refs) - 6
    pairs, (following, _, out, block, mixed, sem) = refs[:splits], refs[splits:]
    rows, page = pairs[0].shape[0], block.shape[1]
    slots = out.shape[0]
    following_place = (info[7] + 1) // 2 % splits
    for slot in range(slots):
        first, count = info[8 + slot], info[8 + slots + slot]

        @pl.when(first + count > rows)
        def _():
            taken = page_rows(rows + page, first, count, page)
            for split in range(splits):
                beyond = following[info[0] ^ split ^ following_place]
                source = jnp.concatenate([pairs[split][...], beyond], axis=0)
                window = jnp.dot(taken, source, preferred_element_type=jnp.float32)
                put_window(block, mixed, 0, pl.multiple_of((info[0] ^ split) * HD, HD), window)
            copy = pltpu.make_async_copy(block.at[0], out.at[slot], sem)
            copy.start()
            copy.wait()


def write_pages(info, pairs):
    rows = pairs[0].shape[0]
    splits = len(pairs)
    slots = rows // PAGE + 3
    return pl.pallas_call(
        page_kernel,
        grid_spec=pltpu.PrefetchScalarGridSpec(
            num_scalar_prefetch=1,
            grid=(splits,),
            in_specs=[pl.BlockSpec((rows, 2 * HD), lambda m, *_: (0, 0))] * splits,
            out_specs=pl.BlockSpec(
                (slots, PAGE, 2, HD), lambda m, info: (0, 0, 0, info[0] ^ m)
            ),
            scratch_shapes=[VMEM((slots, HD // LANES, 2 * PAGE, LANES), jnp.float32)],
        ),
        out_shape=jax.ShapeDtypeStruct((slots, PAGE, 2, splits * HD), jnp.bfloat16),
        compiler_params=pltpu.CompilerParams(vmem_limit_bytes=16 * 2**20),
        cost_estimate=cost(0.3),
        name="pages",
    )(info, *pairs)


def cross_pages(info, pairs, following, written):
    splits = len(pairs)
    smem, here = pl.BlockSpec(memory_space=pltpu.SMEM), pl.BlockSpec(memory_space=pltpu.VMEM)
    anywhere = pl.BlockSpec(memory_space=pl.ANY)
    return pl.pallas_call(
        crossing_kernel,
        in_specs=[smem] + [here] * (splits + 1) + [anywhere],
        out_specs=anywhere,
        out_shape=jax.ShapeDtypeStruct(written.shape, written.dtype),
        input_output_aliases={splits + 2: 0},
        scratch_shapes=[
            VMEM((1, *written.shape[1:]), written.dtype),
            VMEM((1, HD // LANES, 2 * PAGE, LANES), jnp.float32),
            pltpu.SemaphoreType.DMA,
        ],
        compiler_params=pltpu.CompilerParams(vmem_limit_bytes=16 * 2**20),
        cost_estimate=cost(1.5),
        name="crossing",
    )(info, *pairs, following, written)


def out_own_kernel(info, *refs):
    splits = len(refs) - 2
    blocks, (w_own, out) = refs[:splits], refs[splits:]
    total = jnp.zeros(out.shape, jnp.float32)
    for split in range(splits):
        at = pl.ds(pl.multiple_of((info[0] ^ split) * HD, HD), HD)
        total += jnp.dot(blocks[split][...], w_own[at, :], preferred_element_type=jnp.float32)
    out[...] = total


def out_theirs_kernel(info, *refs):
    splits = len(refs) - 5
    blocks, (w_same, w_swap, ours, out, ordered) = refs[:splits], refs[splits:]
    rows = out.shape[0]
    half = splits // 2

    def at(head):
        return pl.ds(pl.multiple_of(head * rows, rows), rows)

    for split, block in enumerate(blocks):
        ordered[at(info[0] ^ split), :] = block[...]
    total = ours[...]
    for weight, core in ((w_same, info[2]), (w_swap, 1 - info[2])):
        for number in range(half):
            total += jnp.dot(
                ordered[at(core * half + number), :],
                weight[number * HD : (number + 1) * HD, :],
                preferred_element_type=jnp.float32,
            )
    out[...] = total.astype(jnp.bfloat16)


def on_chip(kernel, out, name, microseconds, scratch=()):
    here = pl.BlockSpec(memory_space=pltpu.VMEM)
    return lambda info, *operands: pl.pallas_call(
        kernel,
        in_specs=[pl.BlockSpec(memory_space=pltpu.SMEM)] + [here] * len(operands),
        out_specs=jax.tree.map(lambda _: here, out),
        out_shape=out,
        scratch_shapes=scratch,
        compiler_params=pltpu.CompilerParams(vmem_limit_bytes=16 * 2**20),
        cost_estimate=cost(microseconds),
        name=name,
    )(info, *operands)


def split_heads(hidden_in, ln_gain, ln_bias, w_qkv, w_out, segment_ids, prompt_lengths, page_table):
    rows, width = hidden_in.shape
    splits = w_out.shape[0] // HD
    count = lax.axis_size("ctx")
    group = 2 * splits

    def across(value, ctx_mask, tp_mask=0):
        pairs = []
        for c in range(count):
            for t in range(2):
                pairs.append((2 * c + t, 2 * (c ^ ctx_mask) + (t ^ tp_mask)))
        return lax.ppermute(value, ("ctx", "tp"), pairs)

    other = across(hidden_in, 0, 1)
    info, own, gain, bias, *tables, weights, own_columns, outgoing = load(
        splits, prompt_lengths, page_table, hidden_in, ln_gain[None, :], ln_bias[None, :], w_qkv, w_out
    )
    *queries, normed = project(
        query_kernel,
        [(rows, HD)] * splits + [(rows, 2 * width)],
        "queries",
        3.5,
        info,
        own,
        other,
        gain,
        bias,
        *tables,
        weights,
    )
    *pairs, page_head = project(
        pair_kernel,
        [(rows, 2 * HD)] * splits + [(splits, PAGE, 2 * HD)],
        "pairs",
        6,
        info,
        normed,
        *tables,
        weights,
    )

    def after(value, *others):
        return lax.optimization_barrier((value, *others))[0]

    kv_mine = [pairs[0]] + [None] * (splits - 1)
    q_mine = [queries[0]] + [None] * (splits - 1)
    for split in reversed(range(1, splits)):
        q_mine[split] = across(queries[split], 2 * split)
    for split in reversed(range(1, splits)):
        kv_mine[split] = across(pairs[split], 2 * split)
    q_first = on_chip(pick_kernel, jax.ShapeDtypeStruct((rows, HD), jnp.bfloat16), "pick", 0.3)(
        info, *q_mine
    )
    q_tail = lax.ppermute(q_first, "ctx", [(group + 2 * s, 2 * s) for s in range(splits)])
    kv_cache = write_pages(after(info, q_first), pairs)
    *kv_mine[1:], q_tail, kv_cache = lax.optimization_barrier((*kv_mine[1:], q_tail, kv_cache))
    kv_theirs = [across(kv_mine[split], 1) for split in range(splits)]
    w_same = across(after(outgoing, normed), 0, 1)

    tail = on_chip(
        tail_kernel, jax.ShapeDtypeStruct((rows, HD + LANES), jnp.bfloat16), "tail", 2.7
    )(after(info, kv_cache), q_tail, *kv_mine, *kv_theirs)
    w_swap = across(after(w_same, tail), 1)
    far = lax.ppermute(tail, "ctx", [(2 * s, group + 2 * s) for s in range(splits)])
    page_head = after(page_head, tail)
    following = lax.ppermute(page_head, "ctx", [(i, i - 1) for i in range(1, count)])
    gathered, near_mixed, near_level = on_chip(
        main_kernel,
        [
            jax.ShapeDtypeStruct((splits * rows, HD), jnp.bfloat16),
            jax.ShapeDtypeStruct((rows, HD), jnp.float32),
            jax.ShapeDtypeStruct((rows, LANES), jnp.float32),
        ],
        "main",
        4.8,
        [
            VMEM((group * rows, 2 * HD), jnp.bfloat16),
            VMEM((splits * rows, HD), jnp.bfloat16),
        ],
    )(after(info, tail), *q_mine, *kv_mine, *kv_theirs)
    block = jax.ShapeDtypeStruct((rows, HD), jnp.bfloat16)
    blocks = on_chip(merge_kernel, [block] * splits, "merge", 0.6)(
        after(info, w_swap), gathered, near_mixed, near_level, far
    )
    near = [blocks[0]] + [across(blocks[s], 2 * s) for s in range(1, splits)]
    beyond = [across(blocks[s], 2 * s, 1) for s in range(splits)]
    kv_cache = cross_pages(after(info, blocks[0]), pairs, following, kv_cache)
    ours = on_chip(
        out_own_kernel, jax.ShapeDtypeStruct((rows, width), jnp.float32), "out_own", 1.4
    )(info, *near, own_columns)
    attn_out = on_chip(
        out_theirs_kernel,
        jax.ShapeDtypeStruct((rows, width), jnp.bfloat16),
        "out_theirs",
        2,
        [VMEM((splits * rows, HD), jnp.bfloat16)],
    )(info, *beyond, w_same, w_swap, ours)
    return attn_out, kv_cache


def passed_along(value, axis, steps):
    count = lax.axis_size(axis)
    first, last = (max(0, -steps), min(count, count - steps))
    return lax.ppermute(value, axis, [(source, source + steps) for source in range(first, last)])


def normalize(inputs, norm_gain, norm_bias):
    average = jnp.sum(inputs, axis=-1, keepdims=True) / inputs.shape[-1]
    centered = inputs - average
    spread = jnp.sum(centered * centered, axis=-1, keepdims=True) / inputs.shape[-1]
    return centered * lax.rsqrt(spread + EPSILON) * norm_gain + norm_bias


def rotary(inputs, positions):
    quarter = inputs.shape[-1] // 4
    halfway = quarter // 2
    exponent = jnp.arange(0, quarter, 2).astype(jnp.float32) / quarter
    inverse = jnp.power(jnp.float32(10000.0), -exponent)
    angles = positions.astype(jnp.float32)[:, None] * inverse[None, :]
    cosine_table = jnp.concatenate([jnp.cos(angles), jnp.cos(angles)], axis=-1)[:, None, :]
    sine_table = jnp.concatenate([jnp.sin(angles), jnp.sin(angles)], axis=-1)[:, None, :]
    leading = inputs[..., :quarter]
    turned = jnp.concatenate([-leading[..., halfway:], leading[..., :halfway]], axis=-1)
    return jnp.concatenate(
        [leading * cosine_table + turned * sine_table, inputs[..., quarter:]], axis=-1
    )


def segment_positions(segment_rows, row_index, starts):
    table_span = starts.shape[0]
    matches = segment_rows[:, None] == jnp.arange(table_span, dtype=jnp.int32)[None, :]
    first_rows = jnp.sum(jnp.where(matches, starts[None, :], 0), axis=1)
    return row_index - first_rows


def attend(carry_state, query_heads, pair_block, key_marks, query_marks, causal):
    running_max, running_sum, running_acc = carry_state
    scores = jnp.einsum(
        "qhd,khd->hqk", query_heads, pair_block[:, 0], preferred_element_type=jnp.float32
    ) / math.sqrt(query_heads.shape[-1])
    visible = query_marks[:, None] == key_marks[None, :]
    if causal:
        row_count = query_heads.shape[0]
        visible = visible & (jnp.arange(row_count)[None, :] <= jnp.arange(row_count)[:, None])
    scores = jnp.where(visible[None], scores, -jnp.inf)
    newest_max = jnp.maximum(running_max, jnp.max(scores, axis=-1))
    rescale = jnp.exp(running_max - newest_max)
    weights = jnp.exp(scores - newest_max[..., None]).astype(jnp.bfloat16)
    weights = lax.optimization_barrier(weights)
    running_sum = running_sum * rescale + jnp.sum(weights.astype(jnp.float32), axis=-1)
    running_acc = running_acc * rescale[..., None] + jnp.einsum(
        "hqk,khd->hqd", weights, pair_block[:, 1], preferred_element_type=jnp.float32
    )
    return (newest_max, running_sum, running_acc)


def visit_block(carry_state, query_heads, query_marks, pair_block, key_marks):
    tail_mark = key_marks[key_marks.shape[0] - 1]
    relevant = tail_mark == query_marks[0]
    return lax.cond(
        relevant,
        lambda current: attend(current, query_heads, pair_block, key_marks, query_marks, False),
        lambda current: current,
        carry_state,
    )


def relay_pairs(hidden_in, ln_gain, ln_bias, w_qkv, w_out, segment_ids, prompt_lengths, page_table):
    token_rows = hidden_in.shape[0]
    model_width = w_out.shape[1]
    local_heads = w_out.shape[0] // HD
    my_index = lax.axis_index("ctx")
    reach = lax.axis_size("ctx") // 2
    whole_rows = lax.all_gather(hidden_in, "tp", axis=1, tiled=True)
    normed = normalize(whole_rows.astype(jnp.float32), ln_gain, ln_bias).astype(jnp.bfloat16)
    projected = jnp.einsum("td,jdh->tjh", normed, w_qkv, preferred_element_type=jnp.float32)
    starts = jnp.cumsum(prompt_lengths) - prompt_lengths
    row_index = my_index * token_rows + jnp.arange(token_rows, dtype=jnp.int32)
    positions = segment_positions(segment_ids, row_index, starts)
    query_heads = rotary(projected[:, 0].reshape(token_rows, local_heads, HD), positions).astype(
        jnp.bfloat16
    )
    key_heads = rotary(projected[:, 1].reshape(token_rows, local_heads, HD), positions).astype(
        jnp.bfloat16
    )
    value_heads = projected[:, 2].reshape(token_rows, local_heads, HD).astype(jnp.bfloat16)
    pair_block = jnp.stack([key_heads, value_heads], axis=1)
    own_marks = segment_ids + 1
    carry_state = (
        jnp.full((local_heads, token_rows), -jnp.inf, jnp.float32),
        jnp.zeros((local_heads, token_rows), jnp.float32),
        jnp.zeros((local_heads, token_rows, HD), jnp.float32),
    )
    carry_state = attend(carry_state, query_heads, pair_block, own_marks, own_marks, True)

    def relay_step(step, state):
        moving_pair, moving_marks, current = state
        moving_pair, moving_marks = passed_along((moving_pair, moving_marks), "ctx", 1)
        current = visit_block(current, query_heads, own_marks, moving_pair, moving_marks)
        return (moving_pair, moving_marks, current)

    carry_state = lax.fori_loop(0, reach, relay_step, (pair_block, own_marks, carry_state))[2]
    running_max, running_sum, running_acc = carry_state
    attended = (running_acc / running_sum[..., None]).astype(jnp.bfloat16)
    partial_value = jnp.einsum(
        "hqd,hde->qe",
        attended,
        w_out.reshape(local_heads, HD, model_width),
        preferred_element_type=jnp.float32,
    )
    attn_out = lax.psum_scatter(
        partial_value.astype(jnp.bfloat16), "tp", scatter_dimension=1, tiled=True
    )
    tail_pair, tail_marks = passed_along((pair_block[:PAGE], own_marks[:PAGE]), "ctx", -1)
    every_pair = jnp.concatenate([pair_block, tail_pair], axis=0)
    every_marks = jnp.concatenate([own_marks, tail_marks], axis=0)
    every_index = my_index * token_rows + jnp.arange(token_rows + PAGE, dtype=jnp.int32)
    every_segment = jnp.maximum(every_marks - 1, 0)
    every_position = segment_positions(every_segment, every_index, starts)
    page_number = every_position // PAGE
    page_offset = every_position % PAGE
    page_owner = (every_index - page_offset) // token_rows
    is_owned = (every_marks > 0) & (page_owner == my_index)
    page_count = page_table.shape[1]
    table_entry = jnp.take(
        page_table.reshape(-1),
        every_segment * page_count + jnp.clip(page_number, 0, page_count - 1),
    )
    kv_slots = token_rows // PAGE + 3
    target = jnp.where(is_owned, table_entry % kv_slots * PAGE + page_offset, -1)
    placing = (jnp.arange(kv_slots * PAGE, dtype=jnp.int32)[:, None] == target[None, :]).astype(
        jnp.bfloat16
    )
    flat_pair = every_pair.reshape(token_rows + PAGE, 2 * local_heads * HD)
    written = jnp.dot(placing, flat_pair, preferred_element_type=jnp.float32).astype(jnp.bfloat16)
    kv_cache = written.reshape(kv_slots, PAGE, 2, local_heads * HD)
    return (attn_out, kv_cache)


def per_device(*operands):
    heads = operands[4].shape[0] // HD
    spread = lax.axis_size("tp") == 2 and lax.axis_size("ctx") == 4 * heads
    return (split_heads if spread else relay_pairs)(*operands)


def solution(mesh):
    return jax.shard_map(
        per_device,
        mesh=mesh,
        in_specs=(P("ctx", "tp"), P(), P(), P(None, None, "tp"), P("tp", None), P("ctx"), P(), P()),
        out_specs=(P("ctx", "tp"), P("ctx", None, None, "tp")),
        check_vma=False,
    )
```

```python
import functools
import math

import jax
import jax.numpy as jnp
from jax import lax
from jax.experimental import pallas as pl
from jax.experimental.pallas import tpu as pltpu
from jax.sharding import PartitionSpec as P

HD = 256
PAGE = 128
EPSILON = 1e-05
ROT = HD // 4
LANES = 128
PARTS = 16
VMEM = pltpu.VMEM
MASKED = -1e30
LOG2E = 1.4426950408889634


def cost(microseconds):
    return pl.CostEstimate(flops=int(microseconds * 0.35e9), bytes_accessed=0, transcendentals=0)


def row_bounds(info, rows):
    first = jnp.zeros_like(rows)
    for prompt in range(3, 6):
        first = jnp.where(rows >= info[prompt], info[prompt], first)
    return first


def page_windows(info, lengths, table, rows):
    slots = (info.shape[0] - 8) // 2
    for entry in range(8, 8 + 2 * slots):
        info[entry] = 0
    for prompt in range(table.shape[0]):

        def visit(j, carry):
            slot = table[prompt, j] - info[7] * slots
            left = lengths[prompt] - j * PAGE

            @pl.when((slot >= 0) & (slot < slots) & (left > 0))
            def _():
                info[8 + slot] = info[3 + prompt] + j * PAGE - info[7] * rows
                info[8 + slots + slot] = jnp.minimum(left, PAGE)

            return carry

        lax.fori_loop(0, table.shape[1], visit, 0)


def load_kernel(
    splits,
    lengths,
    table,
    own,
    gain,
    bias,
    inverse,
    w_qkv,
    w_out,
    info,
    own_here,
    gain_here,
    bias_here,
    keep,
    below,
    above,
    weights,
    own_columns,
    outgoing,
    sems,
):
    index, rank = lax.axis_index("ctx"), lax.axis_index("tp")
    core = lax.rem(index, 2)
    rows, width = own_here.shape
    send_rows = outgoing.shape[0]

    def columns(place):
        return pl.ds(pl.multiple_of(place * width, width), width)

    sent = pl.ds(pl.multiple_of(core * send_rows, send_rows), send_rows)
    pieces = (
        (own, own_here),
        (gain, gain_here),
        (bias, bias_here),
        (w_qkv, weights),
        (w_out.at[sent, columns(1 - rank)], outgoing),
        (w_out.at[:, columns(rank)], own_columns),
    )
    copies = [pltpu.make_async_copy(*piece, sems.at[i]) for i, piece in enumerate(pieces)]
    for copy in copies:
        copy.start()
    info[0] = lax.rem(index // 2, splits)
    info[1] = rank
    info[2] = core
    info[3] = 0
    info[4] = lengths[0]
    info[5] = lengths[0] + lengths[1]
    info[6] = index // (2 * splits) * (2 * splits * rows)
    info[7] = index
    page_windows(info, lengths, table, rows)
    row = index * rows + lax.broadcasted_iota(jnp.int32, (rows, 1), 0)
    position = (row - row_bounds(info, row)).astype(jnp.float32)
    angles = position * inverse[...]
    cosine, sine = jnp.cos(angles), jnp.sin(angles)
    lane = lax.broadcasted_iota(jnp.int32, cosine.shape, 1)
    keep[...] = jnp.where(lane < ROT, cosine, 1.0)
    below[...] = jnp.where((lane >= ROT // 2) & (lane < ROT), sine, 0.0)
    above[...] = jnp.where(lane < ROT // 2, -sine, 0.0)
    for copy in copies:
        copy.wait()


def load(splits, lengths, page_table, own, gain, bias, w_qkv, w_out):
    rows, width = own.shape
    exponent = jnp.arange(0, ROT, 2).astype(jnp.float32) / ROT
    inverse = jnp.power(jnp.float32(10000.0), -exponent)
    inverse = jnp.tile(inverse, LANES // (ROT // 2))[None, :]
    smem, here = pl.BlockSpec(memory_space=pltpu.SMEM), pl.BlockSpec(memory_space=pltpu.VMEM)
    rotary = jax.ShapeDtypeStruct((rows, LANES), jnp.float32)
    slots = rows // PAGE + 3
    wide = jax.ShapeDtypeStruct(gain.shape, jnp.float32)
    narrow = lambda *shape: jax.ShapeDtypeStruct(shape, jnp.bfloat16)
    return pl.pallas_call(
        functools.partial(load_kernel, splits),
        in_specs=[smem] * 2 + [pl.BlockSpec(memory_space=pltpu.HBM)] * 3 + [here]
        + [pl.BlockSpec(memory_space=pltpu.HBM)] * 2,
        out_specs=[smem] + [here] * 9,
        out_shape=[
            jax.ShapeDtypeStruct((8 + 2 * slots,), jnp.int32),
            narrow(rows, width),
            wide,
            wide,
            rotary,
            rotary,
            rotary,
            narrow(*w_qkv.shape),
            narrow(w_out.shape[0], width),
            narrow(w_out.shape[0] // 2, width),
        ],
        scratch_shapes=[pltpu.SemaphoreType.DMA((6,))],
        compiler_params=pltpu.CompilerParams(vmem_limit_bytes=24 * 2**20),
        cost_estimate=cost(6),
        name="load",
    )(lengths, page_table, own, gain, bias, inverse, w_qkv, w_out)


def normed_rows(info, own, other, gain, bias, normed):
    width = own.shape[1]
    full = 2 * width
    mine = own[...].astype(jnp.float32)
    theirs = other[...].astype(jnp.float32)
    total = jnp.sum(mine, axis=-1, keepdims=True) + jnp.sum(theirs, axis=-1, keepdims=True)
    average = total / full
    mine, theirs = mine - average, theirs - average
    spread = jnp.sum(mine * mine, axis=-1, keepdims=True) + jnp.sum(
        theirs * theirs, axis=-1, keepdims=True
    )
    scale = lax.rsqrt(spread / full + EPSILON)
    for part, place in ((mine, info[1]), (theirs, 1 - info[1])):
        columns = pl.ds(pl.multiple_of(place * width, width), width)
        normed[:, columns] = (part * scale * gain[:, columns] + bias[:, columns]).astype(
            jnp.bfloat16
        )


def turned(inputs, keep, below, above):
    leading = inputs[:, :LANES]
    leading = (
        leading * keep[...]
        + pltpu.roll(leading, ROT // 2, 1) * below[...]
        + pltpu.roll(leading, LANES - ROT // 2, 1) * above[...]
    )
    return jnp.concatenate([leading, inputs[:, LANES:]], axis=1).astype(jnp.bfloat16)


def query_kernel(info, own, other, gain, bias, keep, below, above, weights, *refs):
    queries, normed = refs[:-1], refs[-1]
    normed_rows(info, own, other, gain, bias, normed)
    rows = normed[...]
    for split in reversed(range(len(queries))):
        head = pl.ds(pl.multiple_of((info[0] ^ split) * HD, HD), HD)
        product = jnp.dot(rows, weights[0, :, head], preferred_element_type=jnp.float32)
        queries[split][...] = turned(product, keep, below, above)


def pair_kernel(info, normed, keep, below, above, weights, *refs):
    pairs, head_ref = refs[:-1], refs[-1]
    rows = normed[...]
    for split in reversed(range(len(pairs))):
        head = pl.ds(pl.multiple_of((info[0] ^ split) * HD, HD), HD)
        key = jnp.dot(rows, weights[1, :, head], preferred_element_type=jnp.float32)
        value = jnp.dot(rows, weights[2, :, head], preferred_element_type=jnp.float32)
        pairs[split][:, :HD] = turned(key, keep, below, above)
        pairs[split][:, HD:] = value.astype(jnp.bfloat16)
        head_ref[split] = pairs[split][:PAGE, :]


def project(kernel, outs, name, microseconds, info, *operands):
    here = pl.BlockSpec(memory_space=pltpu.VMEM)
    return pl.pallas_call(
        kernel,
        in_specs=[pl.BlockSpec(memory_space=pltpu.SMEM)] + [here] * len(operands),
        out_specs=[here] * len(outs),
        out_shape=[jax.ShapeDtypeStruct(shape, jnp.bfloat16) for shape in outs],
        compiler_params=pltpu.CompilerParams(vmem_limit_bytes=16 * 2**20),
        cost_estimate=cost(microseconds),
        name=name,
    )(info, *operands)


def softmax_mix(scores, values):
    peak = functools.reduce(
        jnp.maximum, [jnp.max(part, axis=-1, keepdims=True) for part in scores]
    )
    factor = LOG2E / math.sqrt(HD)
    total, mixed = 0.0, 0.0
    for part, value in zip(scores, values):
        weights = jnp.exp2((part - peak) * factor)
        total += jnp.sum(weights, axis=-1, keepdims=True)
        mixed += jnp.dot(
            weights.astype(jnp.bfloat16), value[...], preferred_element_type=jnp.float32
        )
    return mixed / total, peak * factor + jnp.log2(total)


def score(query, keys):
    return lax.dot_general(
        query, keys, (((1,), (1,)), ((), ())), preferred_element_type=jnp.float32
    )


def soft_attend(query, pairs, reach, bounded, causal, base, first_key, last_key):
    cuts = sorted({0, min(bounded, reach), reach - causal, reach})
    scores, values = [], []
    for low, high in zip(cuts, cuts[1:]):
        part = score(query, pairs[low:high, :HD])
        if low < bounded or high > reach - causal:
            column = base + low + lax.broadcasted_iota(jnp.int32, part.shape, 1)
            visible = column >= first_key if low < bounded else column <= last_key
            if low < bounded and high > reach - causal:
                visible = visible & (column <= last_key)
            part = jnp.where(visible, part, MASKED)
        scores.append(part)
        values.append(pairs.at[low:high, HD:])
    return softmax_mix(scores, values)


def pick_kernel(info, *refs):
    for split, ref in enumerate(refs[:-1]):

        @pl.when(info[0] == split)
        def _():
            refs[-1][...] = ref[...]


def tail_kernel(info, *refs):
    splits = (len(refs) - 2) // 2
    query_ref, out = refs[0], refs[-1]
    mine, theirs = refs[1 : splits + 1], refs[splits + 1 : 2 * splits + 1]
    rows = query_ref.shape[0]

    @pl.when((info[6] == 0) & (info[2] == 0))
    def _():
        query = query_ref[...]
        group_rows = 2 * splits * rows
        row = group_rows + lax.broadcasted_iota(jnp.int32, (rows, 1), 0)
        first = row_bounds(info, row)
        scores = []
        for split in range(splits):
            part = score(query, mine[split][:, :HD])
            column = 2 * (info[0] ^ split) * rows + lax.broadcasted_iota(jnp.int32, part.shape, 1)
            scores.append(jnp.where(column >= first, part, MASKED))
        scores += [score(query, ref[:, :HD]) for ref in theirs]
        mixed, level = softmax_mix(scores, [ref.at[:, HD:] for ref in (*mine, *theirs)])
        level = jnp.where(first < group_rows, level, MASKED)
        out[:rows, :] = mixed.astype(jnp.bfloat16)
        level = jnp.broadcast_to(level, (rows, LANES)).T[:PARTS, :]
        part = lax.broadcasted_iota(jnp.int32, (PARTS, rows), 0)
        high = level.astype(jnp.bfloat16).astype(jnp.float32)
        middle = (level - high).astype(jnp.bfloat16).astype(jnp.float32)
        low = level - high - middle
        out[rows:, :] = jnp.where(
            part == 0, high, jnp.where(part == 1, middle, jnp.where(part == 2, low, 0.0))
        ).astype(jnp.bfloat16)


def main_kernel(info, *refs):
    splits = (len(refs) - 5) // 3
    queries, mine, theirs = refs[:splits], refs[splits : 2 * splits], refs[2 * splits : 3 * splits]
    gathered, near_mixed, near_level, pairs, asked = refs[3 * splits :]
    rows = near_mixed.shape[0]

    def at(block):
        return pl.ds(pl.multiple_of(block * rows, rows), rows)

    for split in range(splits):
        place = info[0] ^ split
        asked[at(place), :] = queries[split][...]
        for refs_of, core in ((mine, info[2]), (theirs, 1 - info[2])):
            pairs[at(2 * place + core), :] = refs_of[split][...]
    for place in range(splits):
        row = info[6] + (2 * place + info[2]) * rows + lax.broadcasted_iota(jnp.int32, (rows, 1), 0)
        here = slice(place * rows, (place + 1) * rows)
        mixed, level = soft_attend(
            asked[here, :],
            pairs,
            (2 * place + 2) * rows,
            rows,
            2 * rows,
            info[6],
            row_bounds(info, row),
            row,
        )
        gathered[here, :] = mixed.astype(jnp.bfloat16)
        if place == 0:
            near_mixed[...] = mixed
            near_level[...] = jnp.broadcast_to(level, near_level.shape)


def merge_kernel(info, gathered, near_mixed, near_level, far, *outs):
    rows = near_mixed.shape[0]
    group_rows = 2 * len(outs) * rows
    for split, out in enumerate(outs):
        out[...] = gathered[pl.ds(pl.multiple_of((info[0] ^ split) * rows, rows), rows), :]

    @pl.when((info[6] > 0) & (info[2] == 0))
    def _():
        parts = far[rows:, :].astype(jnp.float32)
        far_level = parts[:1, :] + parts[1:2, :] + parts[2:3, :]
        far_level = jnp.broadcast_to(far_level, (LANES, rows)).T[:, :1]
        level = near_level[:, :1]
        highest = jnp.maximum(level, far_level)
        near_weight, far_weight = jnp.exp2(level - highest), jnp.exp2(far_level - highest)
        mixed = near_mixed[...] * near_weight + far[:rows, :].astype(jnp.float32) * far_weight
        mixed = mixed / (near_weight + far_weight)
        row = group_rows + lax.broadcasted_iota(jnp.int32, (rows, 1), 0)
        mixed = jnp.where(row < info[5], mixed, near_mixed[...]).astype(jnp.bfloat16)
        for split, out in enumerate(outs):

            @pl.when(info[0] == split)
            def _():
                out[...] = mixed


def page_rows(rows, first, count, page):
    target = lax.broadcasted_iota(jnp.int32, (page, rows), 0)
    origin = lax.broadcasted_iota(jnp.int32, (page, rows), 1)
    return ((origin == target + first) & (target < count)).astype(jnp.bfloat16)


def put_window(out, mixed, slot, column, window):
    page = window.shape[0]
    for number, low in enumerate(range(0, HD, LANES)):
        turn = mixed.at[slot, number]
        turn[pl.ds(0, page, stride=2), :] = window[:, low : low + LANES]
        turn[pl.ds(1, page, stride=2), :] = window[:, HD + low : HD + low + LANES]
        out[slot, :, :, pl.ds(column + low, LANES)] = (
            turn[...].astype(jnp.bfloat16).reshape(page, 2, LANES)
        )


def page_kernel(info, *refs):
    splits = len(refs) - 2
    pairs, (out, mixed) = refs[:splits], refs[splits:]
    slots, page = out.shape[:2]
    for number in range(splits):

        @pl.when(pl.program_id(0) == number)
        def _():
            source = pairs[number][...]
            taken = [
                page_rows(source.shape[0], info[8 + slot], info[8 + slots + slot], page)
                for slot in range(slots)
            ]
            windows = jnp.dot(jnp.concatenate(taken), source, preferred_element_type=jnp.float32)
            for slot in range(slots):
                put_window(out, mixed, slot, 0, windows[slot * page : (slot + 1) * page])


def crossing_kernel(info, *refs):
    splits = len(refs) - 6
    pairs, (following, _, out, block, mixed, sem) = refs[:splits], refs[splits:]
    rows, page = pairs[0].shape[0], block.shape[1]
    slots = out.shape[0]
    following_place = (info[7] + 1) // 2 % splits
    for slot in range(slots):
        first, count = info[8 + slot], info[8 + slots + slot]

        @pl.when(first + count > rows)
        def _():
            taken = page_rows(rows + page, first, count, page)
            for split in range(splits):
                beyond = following[info[0] ^ split ^ following_place]
                source = jnp.concatenate([pairs[split][...], beyond], axis=0)
                window = jnp.dot(taken, source, preferred_element_type=jnp.float32)
                put_window(block, mixed, 0, pl.multiple_of((info[0] ^ split) * HD, HD), window)
            copy = pltpu.make_async_copy(block.at[0], out.at[slot], sem)
            copy.start()
            copy.wait()


def write_pages(info, pairs):
    rows = pairs[0].shape[0]
    splits = len(pairs)
    slots = rows // PAGE + 3
    return pl.pallas_call(
        page_kernel,
        grid_spec=pltpu.PrefetchScalarGridSpec(
            num_scalar_prefetch=1,
            grid=(splits,),
            in_specs=[pl.BlockSpec((rows, 2 * HD), lambda m, *_: (0, 0))] * splits,
            out_specs=pl.BlockSpec(
                (slots, PAGE, 2, HD), lambda m, info: (0, 0, 0, info[0] ^ m)
            ),
            scratch_shapes=[VMEM((slots, HD // LANES, 2 * PAGE, LANES), jnp.float32)],
        ),
        out_shape=jax.ShapeDtypeStruct((slots, PAGE, 2, splits * HD), jnp.bfloat16),
        compiler_params=pltpu.CompilerParams(vmem_limit_bytes=16 * 2**20),
        cost_estimate=cost(0.3),
        name="pages",
    )(info, *pairs)


def cross_pages(info, pairs, following, written):
    splits = len(pairs)
    smem, here = pl.BlockSpec(memory_space=pltpu.SMEM), pl.BlockSpec(memory_space=pltpu.VMEM)
    anywhere = pl.BlockSpec(memory_space=pl.ANY)
    return pl.pallas_call(
        crossing_kernel,
        in_specs=[smem] + [here] * (splits + 1) + [anywhere],
        out_specs=anywhere,
        out_shape=jax.ShapeDtypeStruct(written.shape, written.dtype),
        input_output_aliases={splits + 2: 0},
        scratch_shapes=[
            VMEM((1, *written.shape[1:]), written.dtype),
            VMEM((1, HD // LANES, 2 * PAGE, LANES), jnp.float32),
            pltpu.SemaphoreType.DMA,
        ],
        compiler_params=pltpu.CompilerParams(vmem_limit_bytes=16 * 2**20),
        cost_estimate=cost(1.5),
        name="crossing",
    )(info, *pairs, following, written)


def out_own_kernel(info, *refs):
    splits = len(refs) - 2
    blocks, (w_own, out) = refs[:splits], refs[splits:]
    total = jnp.zeros(out.shape, jnp.float32)
    for split in range(splits):
        at = pl.ds(pl.multiple_of((info[0] ^ split) * HD, HD), HD)
        total += jnp.dot(blocks[split][...], w_own[at, :], preferred_element_type=jnp.float32)
    out[...] = total


def out_theirs_kernel(info, *refs):
    splits = len(refs) - 5
    blocks, (w_same, w_swap, ours, out, ordered) = refs[:splits], refs[splits:]
    rows = out.shape[0]
    half = splits // 2

    def at(head):
        return pl.ds(pl.multiple_of(head * rows, rows), rows)

    for split, block in enumerate(blocks):
        ordered[at(info[0] ^ split), :] = block[...]
    total = ours[...]
    for weight, core in ((w_same, info[2]), (w_swap, 1 - info[2])):
        for number in range(half):
            total += jnp.dot(
                ordered[at(core * half + number), :],
                weight[number * HD : (number + 1) * HD, :],
                preferred_element_type=jnp.float32,
            )
    out[...] = total.astype(jnp.bfloat16)


def on_chip(kernel, out, name, microseconds, scratch=()):
    here = pl.BlockSpec(memory_space=pltpu.VMEM)
    return lambda info, *operands: pl.pallas_call(
        kernel,
        in_specs=[pl.BlockSpec(memory_space=pltpu.SMEM)] + [here] * len(operands),
        out_specs=jax.tree.map(lambda _: here, out),
        out_shape=out,
        scratch_shapes=scratch,
        compiler_params=pltpu.CompilerParams(vmem_limit_bytes=16 * 2**20),
        cost_estimate=cost(microseconds),
        name=name,
    )(info, *operands)


def split_heads(hidden_in, ln_gain, ln_bias, w_qkv, w_out, segment_ids, prompt_lengths, page_table):
    rows, width = hidden_in.shape
    splits = w_out.shape[0] // HD
    count = lax.axis_size("ctx")
    group = 2 * splits

    def across(value, ctx_mask, tp_mask=0):
        pairs = []
        for c in range(count):
            for t in range(2):
                pairs.append((2 * c + t, 2 * (c ^ ctx_mask) + (t ^ tp_mask)))
        return lax.ppermute(value, ("ctx", "tp"), pairs)

    other = across(hidden_in, 0, 1)
    info, own, gain, bias, *tables, weights, own_columns, outgoing = load(
        splits, prompt_lengths, page_table, hidden_in, ln_gain[None, :], ln_bias[None, :], w_qkv, w_out
    )
    *queries, normed = project(
        query_kernel,
        [(rows, HD)] * splits + [(rows, 2 * width)],
        "queries",
        3.5,
        info,
        own,
        other,
        gain,
        bias,
        *tables,
        weights,
    )
    *pairs, page_head = project(
        pair_kernel,
        [(rows, 2 * HD)] * splits + [(splits, PAGE, 2 * HD)],
        "pairs",
        6,
        info,
        normed,
        *tables,
        weights,
    )

    def after(value, *others):
        return lax.optimization_barrier((value, *others))[0]

    kv_mine = [pairs[0]] + [None] * (splits - 1)
    q_mine = [queries[0]] + [None] * (splits - 1)
    for split in reversed(range(1, splits)):
        q_mine[split] = across(queries[split], 2 * split)
    for split in reversed(range(1, splits)):
        kv_mine[split] = across(pairs[split], 2 * split)
    q_first = on_chip(pick_kernel, jax.ShapeDtypeStruct((rows, HD), jnp.bfloat16), "pick", 0.3)(
        info, *q_mine
    )
    q_tail = lax.ppermute(q_first, "ctx", [(group + 2 * s, 2 * s) for s in range(splits)])
    kv_cache = write_pages(after(info, q_first), pairs)
    *kv_mine[1:], q_tail, kv_cache = lax.optimization_barrier((*kv_mine[1:], q_tail, kv_cache))
    kv_theirs = [across(kv_mine[split], 1) for split in range(splits)]
    w_same = across(after(outgoing, normed), 0, 1)

    tail = on_chip(
        tail_kernel, jax.ShapeDtypeStruct((rows + PARTS, HD), jnp.bfloat16), "tail", 2.7
    )(after(info, kv_cache), q_tail, *kv_mine, *kv_theirs)
    page_head = after(page_head, tail)
    following = lax.ppermute(page_head, "ctx", [(i, i - 1) for i in range(1, count)])
    far = lax.ppermute(tail, "ctx", [(2 * s, group + 2 * s) for s in range(splits)])
    w_swap = across(after(w_same, tail), 1)
    gathered, near_mixed, near_level = on_chip(
        main_kernel,
        [
            jax.ShapeDtypeStruct((splits * rows, HD), jnp.bfloat16),
            jax.ShapeDtypeStruct((rows, HD), jnp.float32),
            jax.ShapeDtypeStruct((rows, LANES), jnp.float32),
        ],
        "main",
        4.8,
        [
            VMEM((group * rows, 2 * HD), jnp.bfloat16),
            VMEM((splits * rows, HD), jnp.bfloat16),
        ],
    )(after(info, tail), *q_mine, *kv_mine, *kv_theirs)
    block = jax.ShapeDtypeStruct((rows, HD), jnp.bfloat16)
    blocks = on_chip(merge_kernel, [block] * splits, "merge", 0.6)(
        after(info, w_swap), gathered, near_mixed, near_level, far
    )
    near = [blocks[0]] + [across(blocks[s], 2 * s) for s in range(1, splits)]
    beyond = [across(blocks[s], 2 * s, 1) for s in range(splits)]
    kv_cache = cross_pages(after(info, blocks[0]), pairs, following, kv_cache)
    ours = on_chip(
        out_own_kernel, jax.ShapeDtypeStruct((rows, width), jnp.float32), "out_own", 1.4
    )(info, *near, own_columns)
    attn_out = on_chip(
        out_theirs_kernel,
        jax.ShapeDtypeStruct((rows, width), jnp.bfloat16),
        "out_theirs",
        2,
        [VMEM((splits * rows, HD), jnp.bfloat16)],
    )(info, *beyond, w_same, w_swap, ours)
    return attn_out, kv_cache


def passed_along(value, axis, steps):
    count = lax.axis_size(axis)
    first, last = (max(0, -steps), min(count, count - steps))
    return lax.ppermute(value, axis, [(source, source + steps) for source in range(first, last)])


def normalize(inputs, norm_gain, norm_bias):
    average = jnp.sum(inputs, axis=-1, keepdims=True) / inputs.shape[-1]
    centered = inputs - average
    spread = jnp.sum(centered * centered, axis=-1, keepdims=True) / inputs.shape[-1]
    return centered * lax.rsqrt(spread + EPSILON) * norm_gain + norm_bias


def rotary(inputs, positions):
    quarter = inputs.shape[-1] // 4
    halfway = quarter // 2
    exponent = jnp.arange(0, quarter, 2).astype(jnp.float32) / quarter
    inverse = jnp.power(jnp.float32(10000.0), -exponent)
    angles = positions.astype(jnp.float32)[:, None] * inverse[None, :]
    cosine_table = jnp.concatenate([jnp.cos(angles), jnp.cos(angles)], axis=-1)[:, None, :]
    sine_table = jnp.concatenate([jnp.sin(angles), jnp.sin(angles)], axis=-1)[:, None, :]
    leading = inputs[..., :quarter]
    turned = jnp.concatenate([-leading[..., halfway:], leading[..., :halfway]], axis=-1)
    return jnp.concatenate(
        [leading * cosine_table + turned * sine_table, inputs[..., quarter:]], axis=-1
    )


def segment_positions(segment_rows, row_index, starts):
    table_span = starts.shape[0]
    matches = segment_rows[:, None] == jnp.arange(table_span, dtype=jnp.int32)[None, :]
    first_rows = jnp.sum(jnp.where(matches, starts[None, :], 0), axis=1)
    return row_index - first_rows


def attend(carry_state, query_heads, pair_block, key_marks, query_marks, causal):
    running_max, running_sum, running_acc = carry_state
    scores = jnp.einsum(
        "qhd,khd->hqk", query_heads, pair_block[:, 0], preferred_element_type=jnp.float32
    ) / math.sqrt(query_heads.shape[-1])
    visible = query_marks[:, None] == key_marks[None, :]
    if causal:
        row_count = query_heads.shape[0]
        visible = visible & (jnp.arange(row_count)[None, :] <= jnp.arange(row_count)[:, None])
    scores = jnp.where(visible[None], scores, -jnp.inf)
    newest_max = jnp.maximum(running_max, jnp.max(scores, axis=-1))
    rescale = jnp.exp(running_max - newest_max)
    weights = jnp.exp(scores - newest_max[..., None]).astype(jnp.bfloat16)
    weights = lax.optimization_barrier(weights)
    running_sum = running_sum * rescale + jnp.sum(weights.astype(jnp.float32), axis=-1)
    running_acc = running_acc * rescale[..., None] + jnp.einsum(
        "hqk,khd->hqd", weights, pair_block[:, 1], preferred_element_type=jnp.float32
    )
    return (newest_max, running_sum, running_acc)


def visit_block(carry_state, query_heads, query_marks, pair_block, key_marks):
    tail_mark = key_marks[key_marks.shape[0] - 1]
    relevant = tail_mark == query_marks[0]
    return lax.cond(
        relevant,
        lambda current: attend(current, query_heads, pair_block, key_marks, query_marks, False),
        lambda current: current,
        carry_state,
    )


def relay_pairs(hidden_in, ln_gain, ln_bias, w_qkv, w_out, segment_ids, prompt_lengths, page_table):
    token_rows = hidden_in.shape[0]
    model_width = w_out.shape[1]
    local_heads = w_out.shape[0] // HD
    my_index = lax.axis_index("ctx")
    reach = lax.axis_size("ctx") // 2
    whole_rows = lax.all_gather(hidden_in, "tp", axis=1, tiled=True)
    normed = normalize(whole_rows.astype(jnp.float32), ln_gain, ln_bias).astype(jnp.bfloat16)
    projected = jnp.einsum("td,jdh->tjh", normed, w_qkv, preferred_element_type=jnp.float32)
    starts = jnp.cumsum(prompt_lengths) - prompt_lengths
    row_index = my_index * token_rows + jnp.arange(token_rows, dtype=jnp.int32)
    positions = segment_positions(segment_ids, row_index, starts)
    query_heads = rotary(projected[:, 0].reshape(token_rows, local_heads, HD), positions).astype(
        jnp.bfloat16
    )
    key_heads = rotary(projected[:, 1].reshape(token_rows, local_heads, HD), positions).astype(
        jnp.bfloat16
    )
    value_heads = projected[:, 2].reshape(token_rows, local_heads, HD).astype(jnp.bfloat16)
    pair_block = jnp.stack([key_heads, value_heads], axis=1)
    own_marks = segment_ids + 1
    carry_state = (
        jnp.full((local_heads, token_rows), -jnp.inf, jnp.float32),
        jnp.zeros((local_heads, token_rows), jnp.float32),
        jnp.zeros((local_heads, token_rows, HD), jnp.float32),
    )
    carry_state = attend(carry_state, query_heads, pair_block, own_marks, own_marks, True)

    def relay_step(step, state):
        moving_pair, moving_marks, current = state
        moving_pair, moving_marks = passed_along((moving_pair, moving_marks), "ctx", 1)
        current = visit_block(current, query_heads, own_marks, moving_pair, moving_marks)
        return (moving_pair, moving_marks, current)

    carry_state = lax.fori_loop(0, reach, relay_step, (pair_block, own_marks, carry_state))[2]
    running_max, running_sum, running_acc = carry_state
    attended = (running_acc / running_sum[..., None]).astype(jnp.bfloat16)
    partial_value = jnp.einsum(
        "hqd,hde->qe",
        attended,
        w_out.reshape(local_heads, HD, model_width),
        preferred_element_type=jnp.float32,
    )
    attn_out = lax.psum_scatter(
        partial_value.astype(jnp.bfloat16), "tp", scatter_dimension=1, tiled=True
    )
    tail_pair, tail_marks = passed_along((pair_block[:PAGE], own_marks[:PAGE]), "ctx", -1)
    every_pair = jnp.concatenate([pair_block, tail_pair], axis=0)
    every_marks = jnp.concatenate([own_marks, tail_marks], axis=0)
    every_index = my_index * token_rows + jnp.arange(token_rows + PAGE, dtype=jnp.int32)
    every_segment = jnp.maximum(every_marks - 1, 0)
    every_position = segment_positions(every_segment, every_index, starts)
    page_number = every_position // PAGE
    page_offset = every_position % PAGE
    page_owner = (every_index - page_offset) // token_rows
    is_owned = (every_marks > 0) & (page_owner == my_index)
    page_count = page_table.shape[1]
    table_entry = jnp.take(
        page_table.reshape(-1),
        every_segment * page_count + jnp.clip(page_number, 0, page_count - 1),
    )
    kv_slots = token_rows // PAGE + 3
    target = jnp.where(is_owned, table_entry % kv_slots * PAGE + page_offset, -1)
    placing = (jnp.arange(kv_slots * PAGE, dtype=jnp.int32)[:, None] == target[None, :]).astype(
        jnp.bfloat16
    )
    flat_pair = every_pair.reshape(token_rows + PAGE, 2 * local_heads * HD)
    written = jnp.dot(placing, flat_pair, preferred_element_type=jnp.float32).astype(jnp.bfloat16)
    kv_cache = written.reshape(kv_slots, PAGE, 2, local_heads * HD)
    return (attn_out, kv_cache)


def per_device(*operands):
    heads = operands[4].shape[0] // HD
    spread = lax.axis_size("tp") == 2 and lax.axis_size("ctx") == 4 * heads
    return (split_heads if spread else relay_pairs)(*operands)


def solution(mesh):
    return jax.shard_map(
        per_device,
        mesh=mesh,
        in_specs=(P("ctx", "tp"), P(), P(), P(None, None, "tp"), P("tp", None), P("ctx"), P(), P()),
        out_specs=(P("ctx", "tp"), P("ctx", None, None, "tp")),
        check_vma=False,
    )
```
